128 devices in a mesh: section: 16 (over y, z_lo, core), tp: 8 (over x, z_hi).
Axes of the slice: x: 4, y: 4, z: 4 (z_hi: 2, z_lo: 2; z = z_hi * 2 + z_lo), core: 2. Of those that a mesh axis runs over, the one named last changes fastest.
Arguments:
- inputs: bfloat16 [3, 128, 6144], P(None, None, 'tp'), may hold values from -6 to 6
- cotangents: bfloat16 [3, 128, 6144], P(None, None, 'tp'), may hold values from -6 to 6
- carried: bfloat16 [16, 128, 6144], P('section', None, 'tp'), may hold values from -6 to 6
- pending: bfloat16 [16, 128, 6144], P('section', None, 'tp'), may hold values from -6 to 6
- stash: bfloat16 [16, 8, 128, 6144], P('section', None, None, 'tp'), may hold values from -6 to 6
- stash_plan: int32 [16, 4, 2], replicated, may hold values from 0 to 7, as said below
- gain: float32 [16, 6144], P('section'), may hold values from 0.5 to 2
- key_gain: float32 [16, 6144], P('section', 'tp'), may hold values from -4 to 4
- w_value: bfloat16 [16, 6144, 6144], P('section', None, 'tp'), may hold values from -0.078125 to 0.078125
- w_out: bfloat16 [16, 6144, 6144], P('section', 'tp'), may hold values from -0.078125 to 0.078125
Outputs:
- forward_out: bfloat16 [16, 4, 128, 6144], P('section', None, None, 'tp')
- input_grad: bfloat16 [16, 4, 128, 6144], P('section', None, None, 'tp')
The draws below stay inside these ranges and needn't reach their ends.
Inputs may be any that keep to these rules, and one draw needn't show every extreme that they name: stash_plan[s, t, 0] is 0 if the stashed input of section s for step t is held by section s itself and 1 if by section 15 - s; stash_plan[s, t, 1] is its slot in the holder's stash: below 4 for a section's own blocks, 4 or above for blocks of its mirror; no slot of a holder is named twice.
All inputs are finite; a program needn't handle non-finite values.
Results may differ from the reference program's by a relative error of at most 0.034.
Values may be sent and summed in bfloat16 or wider, within the bound.
No kernel may reach another device: no remote copies, remote signals or barrier semaphores. Data moves between devices by JAX's collectives and lax.ppermute only.
A program may use at most 128 MiB of HBM per device.

```python
import math
import jax
import jax.numpy as jnp
from jax import lax

HEAD = 128
D = 6144
TOK = 128
MICRO = 4
SLOTS = 8
SECTIONS = 16
N_TP = 8


def draw_stash_plan(key, part):
    key = jax.random.fold_in(key, 7)
    side_key, order_key = jax.random.split(key, 2)
    orders = jax.vmap(lambda each: jax.random.permutation(each, MICRO))(jax.random.split(order_key, SECTIONS))
    orders = orders.astype(jnp.int32)
    sides = jax.random.randint(side_key, (SECTIONS, MICRO), 0, 2).astype(jnp.int32)
    sides = jnp.where(orders == 0, 0, sides)
    sides = jnp.where(orders == MICRO - 1, 1, sides)
    slots = jnp.where(sides == 0, orders, orders + MICRO)
    return jnp.stack([sides, slots], -1).astype(jnp.int32)


def block_levels(rng, extent, cuts, smallest, high):
    level = 1.0
    for position, shards_of in cuts:
        steps = jax.random.uniform(jax.random.fold_in(jax.random.fold_in(rng, 6), position), (shards_of,), jnp.float32, smallest / len(cuts), high / len(cuts))
        level = level * jnp.repeat(jnp.exp(steps), extent[position] // shards_of).reshape((-1,) + (1,) * (len(extent) - 1 - position))
    return level


def scatter_about(stream_key, extent, deviation, most, pieces=(), kind=jnp.bfloat16):
    entries = jax.random.normal(stream_key, extent, jnp.float32) * deviation
    if len(pieces) > 0:
        entries = block_levels(stream_key, extent, pieces, -0.22, 0.18) * entries
    return jnp.clip(entries, min=-most, max=most).astype(kind)


def setup_inputs(seed: int = 0) -> dict:
    splits = jax.random.split(jax.random.key(seed), 11)
    return {
        "inputs": scatter_about(splits[0], (MICRO - 1, TOK, D), 1.0, 6.0, ((2, 8),)),
        "cotangents": scatter_about(splits[1], (MICRO - 1, TOK, D), 1.0, 6.0, ((2, 8),)),
        "carried": scatter_about(splits[2], (SECTIONS, TOK, D), 1.0, 6.0, ((0, 16), (2, 8))),
        "pending": scatter_about(splits[3], (SECTIONS, TOK, D), 1.0, 6.0, ((0, 16), (2, 8))),
        "stash": scatter_about(splits[4], (SECTIONS, SLOTS, TOK, D), 1.0, 6.0, ((0, 16), (3, 8))),
        "stash_plan": draw_stash_plan(jax.random.fold_in(splits[10], 71), 0),
        "gain": jnp.clip(0.5 + 1.5 * jax.random.uniform(splits[6], (SECTIONS, D), jnp.float32) ** block_levels(splits[6], (SECTIONS, D), ((0, 16),), -0.2, 0.2), 0.5, 2.0),
        "key_gain": scatter_about(splits[7], (SECTIONS, D), 1.0, 4.0, ((0, 16), (1, 8)), jnp.float32),
        "w_value": scatter_about(splits[8], (SECTIONS, D, D), D ** -0.5, 0.078125, ((0, 16), (2, 8))),
        "w_out": scatter_about(splits[9], (SECTIONS, D, D), D ** -0.5, 0.078125, ((0, 16), (1, 8))),
    }


EPSILON = 1e-05

def normalize(block_in, gain_row):
    values32 = block_in.astype(jnp.float32)
    full_width = values32.shape[-1]
    row_mean = lax.optimization_barrier(jnp.sum(values32, -1, keepdims=True)) / full_width
    variance = lax.optimization_barrier(jnp.sum(values32 * values32, -1, keepdims=True)) / full_width - row_mean * row_mean
    inv_std = lax.rsqrt(variance + EPSILON)
    centered = (values32 - row_mean) * inv_std
    normed = (centered * gain_row).astype(jnp.bfloat16)
    return (centered, inv_std, normed)

def attention_probs(normed, key_row):
    token_rows = normed.shape[0]
    queries = normed.reshape(token_rows, -1, HEAD)
    keys_in = (normed.astype(jnp.float32) * key_row).astype(jnp.bfloat16).reshape(token_rows, -1, HEAD)
    scores = jnp.einsum('qhd,khd->hqk', queries.astype(jnp.float32), keys_in.astype(jnp.float32)) / math.sqrt(HEAD)
    causal = jnp.tril(jnp.ones((token_rows, token_rows), dtype=bool))
    scores = jnp.where(causal[None], scores, -1e+30)
    probs = jax.nn.softmax(scores, axis=-1)
    return (queries, keys_in, probs)

def forward_layer(block_in, gain_row, key_row, w_value, w_out):
    token_rows = block_in.shape[0]
    centered, inv_std, normed = normalize(block_in, gain_row)
    values = jnp.dot(normed, w_value, preferred_element_type=jnp.float32).astype(jnp.bfloat16)
    queries, keys_in, probs = attention_probs(normed, key_row)
    weights_bf = probs.astype(jnp.bfloat16)
    mixed = jnp.einsum('hqk,khd->qhd', weights_bf.astype(jnp.float32), values.reshape(token_rows, -1, HEAD).astype(jnp.float32)).astype(jnp.bfloat16)
    share = w_out.shape[0] // N_TP
    partial_out = jnp.einsum('tgc,gcd->gtd', mixed.reshape(token_rows, N_TP, share).astype(jnp.float32), w_out.reshape(N_TP, share, -1).astype(jnp.float32))
    head_sum = lax.optimization_barrier(jnp.sum(partial_out.astype(jnp.bfloat16).astype(jnp.float32), 0))
    return (block_in.astype(jnp.float32) + head_sum).astype(jnp.bfloat16)

def backward_layer(block_in, grad_in, gain_row, key_row, w_value, w_out):
    token_rows = block_in.shape[0]
    full_width = block_in.shape[1]
    centered, inv_std, normed = normalize(block_in, gain_row)
    values = jnp.dot(normed, w_value, preferred_element_type=jnp.float32).astype(jnp.bfloat16)
    queries, keys_in, probs = attention_probs(normed, key_row)
    weights_bf = probs.astype(jnp.bfloat16)
    grad_attn = jnp.dot(grad_in, w_out.T, preferred_element_type=jnp.float32).astype(jnp.bfloat16)
    grad_attn = grad_attn.reshape(token_rows, -1, HEAD)
    values3 = values.reshape(token_rows, -1, HEAD)
    grad_probs = jnp.einsum('qhd,khd->hqk', grad_attn.astype(jnp.float32), values3.astype(jnp.float32))
    grad_values = jnp.einsum('hqk,qhd->khd', weights_bf.astype(jnp.float32), grad_attn.astype(jnp.float32)).astype(jnp.bfloat16)
    grad_scores = (probs * (grad_probs - lax.optimization_barrier(jnp.sum(grad_probs * probs, -1, keepdims=True))) / math.sqrt(HEAD)).astype(jnp.bfloat16)
    grad_query = jnp.einsum('hqk,khd->qhd', grad_scores.astype(jnp.float32), keys_in.astype(jnp.float32))
    grad_keys = jnp.einsum('hqk,qhd->khd', grad_scores.astype(jnp.float32), queries.astype(jnp.float32))
    grad_direct = grad_query.reshape(token_rows, -1) + grad_keys.reshape(token_rows, -1) * key_row
    share = full_width // N_TP
    partial_in = jnp.einsum('tgc,dgc->gtd', grad_values.reshape(token_rows, N_TP, share).astype(jnp.float32), w_value.reshape(full_width, N_TP, share).astype(jnp.float32))
    grad_normed = lax.optimization_barrier(jnp.sum(partial_in.astype(jnp.bfloat16).astype(jnp.float32), 0)) + grad_direct
    grad_scaled = grad_normed * gain_row
    first_mean = lax.optimization_barrier(jnp.sum(grad_scaled, -1, keepdims=True)) / full_width
    second_mean = lax.optimization_barrier(jnp.sum(grad_scaled * centered, -1, keepdims=True)) / full_width
    grad_block = inv_std * (grad_scaled - first_mean - centered * second_mean)
    return (grad_in.astype(jnp.float32) + grad_block).astype(jnp.bfloat16)

def reference(inputs, cotangents, carried, pending, stash, stash_plan, gain, key_gain, w_value, w_out):
    section_ids = jnp.arange(SECTIONS, dtype=jnp.int32)
    fwd_input = carried
    grad_input = pending
    forward_list = []
    backward_list = []
    for step_index in range(MICRO):
        outputs_now = lax.map(lambda pack: forward_layer(*pack), (fwd_input, gain, key_gain, w_value, w_out))
        holder = jnp.where(stash_plan[:, step_index, 0] == 0, section_ids, SECTIONS - 1 - section_ids).astype(jnp.int32)
        blocks = stash[holder, stash_plan[:, step_index, 1].astype(jnp.int32)]
        grads_now = lax.map(lambda pack: backward_layer(*pack), (blocks, grad_input, gain, key_gain, w_value, w_out))
        forward_list.append(outputs_now)
        backward_list.append(grads_now)
        if step_index + 1 < MICRO:
            fwd_input = jnp.concatenate([inputs[step_index][None], outputs_now[:-1]], 0)
            grad_input = jnp.concatenate([grads_now[1:], cotangents[step_index][None]], 0)
    return (jnp.stack(forward_list, 1), jnp.stack(backward_list, 1))
```

```python
import math

import jax
import jax.numpy as jnp
from jax import lax
from jax.experimental import pallas as pl
from jax.experimental.pallas import tpu as pltpu
from jax.sharding import PartitionSpec as P

HEAD = 128
EPSILON = 1e-05
RINGX = 4
PEERS = 8
BF16 = jnp.bfloat16
F32 = jnp.float32
NT = (((1,), (1,)), ((), ()))
NN = (((1,), (0,)), ((), ()))
TN = (((0,), (0,)), ((), ()))
VMEM = pl.BlockSpec(memory_space=pltpu.VMEM)
SMEM = pl.BlockSpec(memory_space=pltpu.SMEM)


def params():
    return pltpu.CompilerParams(
        dimension_semantics=("arbitrary",), vmem_limit_bytes=24 * 1024 * 1024
    )


def cost(flops, nbytes):
    return pl.CostEstimate(flops=flops, bytes_accessed=nbytes, transcendentals=0)


def place(i, dx, dz):
    return ((i // 2 + dx) % RINGX) * 2 + ((i % 2) ^ dz)


def shift(array, dx, dz):
    return lax.ppermute(array, "tp", [(i, place(i, dx, dz)) for i in range(PEERS)])


def from_behind(array, by):
    peers = lax.axis_size("section")
    pairs = [(i, i + by) for i in range(peers) if 0 <= i + by < peers]
    return lax.ppermute(array, "section", pairs)


def gather(own, axis):
    partner = shift(own, 0, 1)
    pair = jnp.stack([own, partner])
    behind = shift(pair, -1, 0)
    ahead = shift(pair, 1, 0)
    half = pair.shape[axis] // 2
    first = shift(lax.slice_in_dim(behind, 0, half, axis=axis), -1, 0)
    second = shift(lax.slice_in_dim(ahead, half, 2 * half, axis=axis), 1, 0)
    return own, partner, behind, first, second, ahead


def scatter_sum(here, far_first, far_second, plus, minus, axis):
    half = far_first.shape[axis]
    got_first = shift(far_first, 1, 0)
    got_second = shift(far_second, -1, 0)

    def add(a, b):
        return (a.astype(F32) + b.astype(F32)).astype(BF16)

    plus = jnp.concatenate(
        [
            add(lax.slice_in_dim(plus, 0, half, axis=axis), got_first),
            lax.slice_in_dim(plus, half, 2 * half, axis=axis),
        ],
        axis,
    )
    minus = jnp.concatenate(
        [
            lax.slice_in_dim(minus, 0, half, axis=axis),
            add(lax.slice_in_dim(minus, half, 2 * half, axis=axis), got_second),
        ],
        axis,
    )
    got_plus = shift(plus, 1, 0)
    got_minus = shift(minus, -1, 0)
    total = here.astype(F32) + got_plus.astype(F32) + got_minus.astype(F32)
    return total[0] + shift(total[1].astype(BF16), 0, 1).astype(F32)


def softmax_scores(queries, keys, tokens):
    scores = lax.dot_general(queries, keys, NT, preferred_element_type=F32) / math.sqrt(HEAD)
    rows = lax.broadcasted_iota(jnp.int32, (tokens, tokens), 0)
    columns = lax.broadcasted_iota(jnp.int32, (tokens, tokens), 1)
    scores = jnp.where(columns <= rows, scores, -1e30)
    raised = jnp.exp(scores - jnp.max(scores, -1, keepdims=True))
    return raised / jnp.sum(raised, -1, keepdims=True)


def layer_body(stashed, tokens, width, *refs):
    idx, own, partner, plus, far_first, far_second, minus, gain, key_row, weight = refs[:10]
    if stashed:
        out_values, out_probs, out_normed, out_centered, out_inv = refs[10:15]
    else:
        (out_mixed,) = refs[10:11]
    pieces, total, normed_own, mean_ref, inv_ref = refs[-5:]
    step = pl.program_id(0)
    half = tokens // 2
    full = width * PEERS

    @pl.when(step == 0)
    def _():
        pieces[0] = own[...]
        pieces[1] = partner[...]
        pieces[2:4] = plus[...]
        pieces[4:6, :half] = far_first[...]
        pieces[4:6, half:] = far_second[...]
        pieces[6:8] = minus[...]
        sums = jnp.zeros((tokens, HEAD), F32)
        squares = jnp.zeros((tokens, HEAD), F32)
        for r in range(PEERS):
            for c in range(width // HEAD):
                x = pieces[r, :, c * HEAD : (c + 1) * HEAD].astype(F32)
                sums += x
                squares += x * x
        mean = jnp.sum(sums, -1, keepdims=True) / full
        variance = jnp.sum(squares, -1, keepdims=True) / full - mean * mean
        mean_ref[...] = jnp.broadcast_to(mean, (tokens, HEAD))
        inv_ref[...] = jnp.broadcast_to(lax.rsqrt(variance + EPSILON), (tokens, HEAD))
        total[...] = jnp.zeros_like(total)

    centered = (pieces[step].astype(F32) - mean_ref[:, :1]) * inv_ref[:, :1]
    normed = (centered * gain[0]).astype(BF16)

    @pl.when(step == 0)
    def _():
        normed_own[...] = normed

    total[...] += lax.dot_general(normed, weight[...], NN, preferred_element_type=F32)

    if stashed:
        share = tokens // PEERS
        rows = pl.ds(pl.multiple_of(idx[0] * share, share), share)
        out_centered[...] = (pieces[step, rows, :].astype(F32) - mean_ref[rows, :1]) * inv_ref[
            rows, :1
        ]

        @pl.when(step == 0)
        def _():
            out_inv[...] = inv_ref[rows, :]

    @pl.when(step == PEERS - 1)
    def _():
        values = total[...].astype(BF16)
        if stashed:
            out_values[...] = values
            out_normed[...] = normed_own[...]
        for h in range(width // HEAD):
            part = slice(h * HEAD, (h + 1) * HEAD)
            queries = normed_own[:, part]
            keys = (queries.astype(F32) * key_row[:, part]).astype(BF16)
            probs = softmax_scores(queries, keys, tokens)
            if stashed:
                out_probs[h] = probs
            else:
                out_mixed[:, part] = lax.dot_general(
                    probs.astype(BF16), values[:, part], NN, preferred_element_type=F32
                ).astype(BF16)


def layer_call(stashed, idx, pieces, gain, key_row, weight):
    tokens, width = pieces[0].shape
    full = width * PEERS
    share = tokens // PEERS
    if stashed:
        out_shape = (
            jax.ShapeDtypeStruct((tokens, width), BF16),
            jax.ShapeDtypeStruct((width // HEAD, tokens, tokens), F32),
            jax.ShapeDtypeStruct((tokens, width), BF16),
            jax.ShapeDtypeStruct((share, full), F32),
            jax.ShapeDtypeStruct((share, HEAD), F32),
        )
        out_specs = (
            pl.BlockSpec((tokens, width), lambda r, idx: (0, 0)),
            pl.BlockSpec((width // HEAD, tokens, tokens), lambda r, idx: (0, 0, 0)),
            pl.BlockSpec((tokens, width), lambda r, idx: (0, 0)),
            pl.BlockSpec((share, width), lambda r, idx: (0, idx[r])),
            pl.BlockSpec((share, HEAD), lambda r, idx: (0, 0)),
        )
    else:
        out_shape = jax.ShapeDtypeStruct((tokens, width), BF16)
        out_specs = pl.BlockSpec((tokens, width), lambda r, idx: (0, 0))

    def body(*refs):
        layer_body(stashed, tokens, width, *refs)

    def whole(array):
        zeros = (0,) * array.ndim
        return pl.BlockSpec(array.shape, lambda r, idx: zeros)

    return pl.pallas_call(
        body,
        out_shape=out_shape,
        grid_spec=pltpu.PrefetchScalarGridSpec(
            num_scalar_prefetch=1,
            grid=(PEERS,),
            in_specs=[whole(p) for p in pieces]
            + [
                pl.BlockSpec((1, 1, width), lambda r, idx: (idx[r], 0, 0)),
                whole(key_row),
                pl.BlockSpec((width, width), lambda r, idx: (idx[r], 0)),
            ],
            out_specs=out_specs,
            scratch_shapes=[
                pltpu.VMEM((PEERS, tokens, width), BF16),
                pltpu.VMEM((tokens, width), F32),
                pltpu.VMEM((tokens, width), BF16),
                pltpu.VMEM((tokens, HEAD), F32),
                pltpu.VMEM((tokens, HEAD), F32),
            ],
        ),
        compiler_params=params(),
        cost_estimate=cost(2 * tokens * full * width, 2 * full * width),
        name="stash_layer" if stashed else "mix_layer",
    )(idx, *pieces, gain, key_row, weight)


def far_call(idx, mixed, weight):
    tokens, width = mixed.shape

    def body(idx, mixed, weight, first, second):
        product = lax.dot_general(
            mixed[...], weight[...], NN, preferred_element_type=F32
        ).astype(BF16)
        first[0] = product[: tokens // 2]
        second[0] = product[tokens // 2 :]

    half = pl.BlockSpec((1, tokens // 2, width), lambda r, idx: (r, 0, 0))
    return pl.pallas_call(
        body,
        out_shape=[jax.ShapeDtypeStruct((2, tokens // 2, width), BF16)] * 2,
        grid_spec=pltpu.PrefetchScalarGridSpec(
            num_scalar_prefetch=1,
            grid=(2,),
            in_specs=[
                pl.BlockSpec((tokens, width), lambda r, idx: (0, 0)),
                pl.BlockSpec((width, width), lambda r, idx: (0, idx[4 + r])),
            ],
            out_specs=[half, half],
        ),
        compiler_params=params(),
        cost_estimate=cost(4 * tokens * width * width, 4 * width * width),
        name="project_far",
    )(idx, mixed, weight)


def near_call(idx, mixed, weight):
    tokens, width = mixed.shape

    def order(r, idx):
        return idx[lax.select(r < 2, r + 2, lax.select(r < 4, r + 4, r - 4))]

    def body(idx, mixed, weight, plus, minus, here):
        step = pl.program_id(0)
        product = lax.dot_general(
            mixed[...], weight[...], NN, preferred_element_type=F32
        ).astype(BF16)

        @pl.when(step < 2)
        def _():
            plus[0] = product

        @pl.when((step >= 2) & (step < 4))
        def _():
            minus[0] = product

        @pl.when(step >= 4)
        def _():
            here[0] = product

    def pair(first):
        return pl.BlockSpec(
            (1, tokens, width), lambda r, idx: (jnp.clip(r - first, 0, 1), 0, 0)
        )

    return pl.pallas_call(
        body,
        out_shape=[jax.ShapeDtypeStruct((2, tokens, width), BF16)] * 3,
        grid_spec=pltpu.PrefetchScalarGridSpec(
            num_scalar_prefetch=1,
            grid=(6,),
            in_specs=[
                pl.BlockSpec((tokens, width), lambda r, idx: (0, 0)),
                pl.BlockSpec((width, width), lambda r, idx: (0, order(r, idx))),
            ],
            out_specs=[pair(0), pair(2), pair(4)],
        ),
        compiler_params=params(),
        cost_estimate=cost(12 * tokens * width * width, 12 * width * width),
        name="project_near",
    )(idx, mixed, weight)


def attention_grad_call(idx, pieces, stashed, key_row, weight):
    share, full = pieces[0].shape
    tokens = share * PEERS
    width = full // PEERS
    values, probs, normed = stashed

    def body(
        idx, own, partner, plus, far_first, far_second, minus, values, probs, normed, key_row,
        weight, out_values, out_direct, grads, total, sort_values, sort_direct,
    ):
        step = pl.program_id(0)

        def rows(r):
            return pl.ds(pl.multiple_of(idx[r] * share, share), share)

        @pl.when(step == 0)
        def _():
            grads[rows(0)] = own[...]
            grads[rows(1)] = partner[...]
            for dz in range(2):
                grads[rows(2 + dz)] = plus[dz]
                grads[rows(4 + dz), : full // 2] = far_first[dz]
                grads[rows(4 + dz), full // 2 :] = far_second[dz]
                grads[rows(6 + dz)] = minus[dz]
            total[...] = jnp.zeros_like(total)

        columns = pl.ds(pl.multiple_of(step * width, HEAD), width)
        total[...] += lax.dot_general(
            grads[:, columns], weight[...], NT, preferred_element_type=F32
        )

        @pl.when(step == PEERS - 1)
        def _():
            for h in range(width // HEAD):
                part = slice(h * HEAD, (h + 1) * HEAD)
                grad_mixed = total[:, part].astype(BF16)
                weights = probs[h]
                grad_probs = lax.dot_general(
                    grad_mixed, values[:, part], NT, preferred_element_type=F32
                )
                grad_values = lax.dot_general(
                    weights.astype(BF16), grad_mixed, TN, preferred_element_type=F32
                )
                grad_scores = (
                    weights
                    * (grad_probs - jnp.sum(grad_probs * weights, -1, keepdims=True))
                    / math.sqrt(HEAD)
                ).astype(BF16)
                queries = normed[:, part]
                keys = (queries.astype(F32) * key_row[:, part]).astype(BF16)
                grad_query = lax.dot_general(grad_scores, keys, NN, preferred_element_type=F32)
                grad_keys = lax.dot_general(grad_scores, queries, TN, preferred_element_type=F32)
                sort_values[:, part] = grad_values.astype(BF16)
                sort_direct[:, part] = grad_query + grad_keys * key_row[:, part]
            for r in range(PEERS):
                out_values[r * share : (r + 1) * share] = sort_values[rows(r)]
                out_direct[r * share : (r + 1) * share] = sort_direct[rows(r)]

    def whole(array):
        zeros = (0,) * array.ndim
        return pl.BlockSpec(array.shape, lambda r, idx: zeros)

    result = pl.BlockSpec((tokens, width), lambda r, idx: (0, 0))
    return pl.pallas_call(
        body,
        out_shape=(
            jax.ShapeDtypeStruct((tokens, width), BF16),
            jax.ShapeDtypeStruct((tokens, width), F32),
        ),
        grid_spec=pltpu.PrefetchScalarGridSpec(
            num_scalar_prefetch=1,
            grid=(PEERS,),
            in_specs=[whole(p) for p in pieces]
            + [whole(values), whole(probs), whole(normed), whole(key_row)]
            + [pl.BlockSpec((width, width), lambda r, idx: (0, r))],
            out_specs=(result, result),
            scratch_shapes=[
                pltpu.VMEM((tokens, full), BF16),
                pltpu.VMEM((tokens, width), F32),
                pltpu.VMEM((tokens, width), BF16),
                pltpu.VMEM((tokens, width), F32),
            ],
        ),
        compiler_params=params(),
        cost_estimate=cost(2 * tokens * full * width, 2 * full * width),
        name="attention_grad",
    )(idx, *pieces, values, probs, normed, key_row, weight)


def back_project_call(idx, grad_values, direct, weight):
    tokens, width = grad_values.shape
    full = width * PEERS
    share = tokens // PEERS

    def body(idx, grad_values, direct, weight, here, plus, far_first, far_second, minus):
        step = pl.program_id(0)
        product = lax.dot_general(
            grad_values[...], weight[...], NT, preferred_element_type=F32
        )
        mine = (step == idx[0]).astype(F32)
        product = (product + direct[...] * mine).astype(BF16)

        def piece(r):
            return product[r * share : (r + 1) * share]

        for dz in range(2):
            here[dz] = piece(dz)
            plus[dz] = piece(2 + dz)
            minus[dz] = piece(6 + dz)

        @pl.when(step < PEERS // 2)
        def _():
            for dz in range(2):
                far_first[dz] = piece(4 + dz)

        @pl.when(step >= PEERS // 2)
        def _():
            for dz in range(2):
                far_second[dz] = piece(4 + dz)

    part = pl.BlockSpec((2, share, width), lambda c, idx: (0, 0, c))
    return pl.pallas_call(
        body,
        out_shape=[
            jax.ShapeDtypeStruct((2, share, full // (2 if k in (2, 3) else 1)), BF16)
            for k in range(5)
        ],
        grid_spec=pltpu.PrefetchScalarGridSpec(
            num_scalar_prefetch=1,
            grid=(PEERS,),
            in_specs=[
                pl.BlockSpec((tokens, width), lambda c, idx: (0, 0)),
                pl.BlockSpec((tokens, width), lambda c, idx: (0, 0)),
                pl.BlockSpec((width, width), lambda c, idx: (c, 0)),
            ],
            out_specs=[
                part,
                part,
                pl.BlockSpec((2, share, width), lambda c, idx: (0, 0, jnp.minimum(c, 3))),
                pl.BlockSpec((2, share, width), lambda c, idx: (0, 0, jnp.maximum(c - 4, 0))),
                part,
            ],
        ),
        compiler_params=params(),
        cost_estimate=cost(2 * tokens * full * width, 2 * full * width),
        name="back_project",
    )(idx, grad_values, direct, weight)


def to_tokens(array):
    return lax.all_to_all(array, "tp", split_axis=1, concat_axis=2, tiled=True)


def to_features(array):
    return lax.all_to_all(array, "tp", split_axis=2, concat_axis=1, tiled=True)


def per_device(
    inputs, cotangents, carried, pending, stash, stash_plan, gain, key_gain, w_value, w_out
):
    steps = inputs.shape[0] + 1
    width = key_gain.shape[-1]
    full = gain.shape[-1]
    me = lax.axis_index("tp")
    idx = jnp.stack([place(me, r // 2, r % 2) for r in range(PEERS)]).astype(jnp.int32)
    section = lax.axis_index("section")
    sections = lax.axis_size("section")
    mirror = sections - 1 - section
    gain_full = gain[0]
    gain_blocks = gain[0].reshape(PEERS, 1, width)
    value_local = w_value[0]
    out_local = w_out[0]
    held = stash[0]

    def stashed_inputs(first, last):
        sending = jnp.stack([held[stash_plan[mirror, t, 1]] for t in range(first, last)])
        got = lax.ppermute(sending, "section", [(i, sections - 1 - i) for i in range(sections)])
        return [
            jnp.where(
                stash_plan[section, t, 0] == 0, held[stash_plan[section, t, 1]], got[t - first]
            )
            for t in range(first, last)
        ]

    stash_in = stashed_inputs(0, 1) + stashed_inputs(1, steps)
    grad_tokens = to_tokens(jnp.concatenate([pending, cotangents], 0))

    fwd_input = carried[0]
    grad_input = grad_tokens[0]
    forward_list = []
    backward_list = []
    for t in range(steps):
        if t > 0:
            received = from_behind(forward_list[-1], 1)
            fwd_input = jnp.where(section == 0, inputs[t - 1], received)
            received_grad = from_behind(backward_list[-1], -1)
            grad_input = jnp.where(section == sections - 1, grad_tokens[t], received_grad)
        mixed = layer_call(
            False, idx, gather(fwd_input, 1), gain_blocks, key_gain, value_local
        )
        far_first, far_second = far_call(idx, mixed, out_local)
        plus, minus, here = near_call(idx, mixed, out_local)
        head_sum = scatter_sum(here, far_first, far_second, plus, minus, 1)
        forward_list.append((fwd_input.astype(F32) + head_sum).astype(BF16))

        values, probs, normed, centered, inv_std = layer_call(
            True, idx, gather(stash_in[t], 1), gain_blocks, key_gain, value_local
        )
        grad_values, direct = attention_grad_call(
            idx, gather(grad_input, 2), (values, probs, normed), key_gain, out_local
        )
        here, plus, far_first, far_second, minus = back_project_call(
            idx, grad_values, direct, value_local
        )
        grad_normed = scatter_sum(here, far_first, far_second, plus, minus, 2)
        grad_scaled = grad_normed * gain_full
        first_mean = jnp.sum(grad_scaled, -1, keepdims=True) / full
        second_mean = jnp.sum(grad_scaled * centered, -1, keepdims=True) / full
        grad_block = inv_std[:, :1] * (grad_scaled - first_mean - centered * second_mean)
        backward_list.append((grad_input.astype(F32) + grad_block).astype(BF16))
    backward = jnp.concatenate(
        [to_features(jnp.stack(backward_list[:-1])), to_features(backward_list[-1][None])]
    )
    return (jnp.stack(forward_list, 0)[None], backward[None])


def solution(mesh):
    return jax.shard_map(
        per_device,
        mesh=mesh,
        in_specs=(
            P(None, None, "tp"),
            P(None, None, "tp"),
            P("section", None, "tp"),
            P("section", None, "tp"),
            P("section", None, None, "tp"),
            P(),
            P("section", None),
            P("section", "tp"),
            P("section", None, "tp"),
            P("section", "tp", None),
        ),
        out_specs=(P("section", None, None, "tp"), P("section", None, None, "tp")),
        check_vma=False,
    )
```

```python
import math

import jax
import jax.numpy as jnp
from jax import lax
from jax.experimental import pallas as pl
from jax.experimental.pallas import tpu as pltpu
from jax.sharding import PartitionSpec as P

HEAD = 128
EPSILON = 1e-05
RINGX = 4
PEERS = 8
BF16 = jnp.bfloat16
VMEM_LIMIT = 46 * 1024 * 1024
F32 = jnp.float32
HBM = pl.BlockSpec(memory_space=pl.ANY)
NT = (((1,), (1,)), ((), ()))
NN = (((1,), (0,)), ((), ()))
TN = (((0,), (0,)), ((), ()))


def params():
    return pltpu.CompilerParams(
        dimension_semantics=("arbitrary",), vmem_limit_bytes=VMEM_LIMIT
    )


def cost(flops, nbytes):
    return pl.CostEstimate(flops=1, bytes_accessed=1, transcendentals=0)


def place(i, dx, dz):
    return ((i // 2 + dx) % RINGX) * 2 + ((i % 2) ^ dz)


def shift(array, dx, dz):
    return lax.ppermute(array, "tp", [(i, place(i, dx, dz)) for i in range(PEERS)])


def hop(array, by, cross):
    peers = lax.axis_size("section")
    pairs = [
        (i * PEERS + j, (i + by) * PEERS + (j ^ cross))
        for i in range(peers)
        if 0 <= i + by < peers
        for j in range(PEERS)
    ]
    return lax.ppermute(array, ("section", "tp"), pairs)


def partner_in(array, section):
    pairs = [(section * PEERS + j, section * PEERS + (j ^ 1)) for j in range(PEERS)]
    return lax.ppermute(array, ("section", "tp"), pairs)


def add(a, b):
    return (a.astype(F32) + b.astype(F32)).astype(BF16)


class Order:
    def __init__(self):
        self.token = jnp.zeros((), F32)

    def pin(self, *arrays):
        self.token, *arrays = lax.optimization_barrier((self.token, *arrays))
        return arrays if len(arrays) > 1 else arrays[0]


class Gather:
    def __init__(self, order, pair):
        self.order = order
        self.pair = order.pin(pair)
        far = shift(self.pair, 2, 0)
        self.rest = shift(self.pair, -1, 0), far, shift(self.pair, 1, 0)

    def done(self):
        return self.pair, *self.order.pin(*self.rest)


class ScatterSum:
    def __init__(self, order, far, plus, minus):
        self.order = order
        far, plus, minus = order.pin(far, plus, minus)
        self.got = shift(far, 2, 0), shift(plus, 1, 0), shift(minus, -1, 0)

    def done(self):
        return self.order.pin(*self.got)


class Hop:
    def __init__(self, order, part, by):
        self.order = order
        part = order.pin(part)
        self.got = hop(part, by, 0), hop(part, by, 1)

    def done(self, at_edge, edge_pair):
        same, cross = self.order.pin(*self.got)
        return jnp.where(at_edge, edge_pair, add(same, cross[::-1]))


def whole(array):
    zeros = (0,) * array.ndim
    return pl.BlockSpec(array.shape, lambda r, idx: zeros)


def per_head(heads, product):
    return jnp.concatenate([product(slice(h * HEAD, (h + 1) * HEAD)) for h in range(heads)], 0)


def softmax_scores(queries, keys, tokens, heads):
    scores = per_head(
        heads,
        lambda p: lax.dot_general(queries[:, p], keys[:, p], NT, preferred_element_type=F32),
    )
    scores = scores / math.sqrt(HEAD)
    rows = lax.broadcasted_iota(jnp.int32, scores.shape, 0) % tokens
    columns = lax.broadcasted_iota(jnp.int32, scores.shape, 1)
    scores = jnp.where(columns <= rows, scores, -1e30)
    raised = jnp.exp(scores - jnp.max(scores, -1, keepdims=True))
    return raised / jnp.sum(raised, -1, keepdims=True)


def row_block(tiles, k):
    return tiles.at[k]


def column_block(tiles, k):
    return tiles.at[PEERS + k]


def tile_call(w_value, w_out):
    width = w_value.shape[1]

    def body(w_value, w_out, tiles):
        tiles[0, 0] = w_value[...]
        tiles[1, 0] = w_out[...]

    tiles = pl.pallas_call(
        body,
        out_shape=jax.ShapeDtypeStruct((2, PEERS, width, width), BF16),
        grid=(PEERS,),
        in_specs=[
            pl.BlockSpec((width, width), lambda k: (k, 0)),
            pl.BlockSpec((width, width), lambda k: (0, k)),
        ],
        out_specs=pl.BlockSpec((2, 1, width, width), lambda k: (0, k, 0, 0)),
        compiler_params=params(),
        cost_estimate=cost(1, 1),
        name="weight_tiles",
    )(w_value, w_out)
    return tiles.reshape(2 * PEERS, width, width)


def stream_scratch(count, width):
    return [pltpu.VMEM((count, width, width), BF16), pltpu.SemaphoreType.DMA((count,))]


def wait_block(weight, blocks, sems, step, block_of):
    pltpu.make_async_copy(block_of(weight, 0), blocks.at[step], sems.at[step]).wait()


def layer_body(stashed, natural, tokens, width, *refs):
    idx = refs[0]
    if natural:
        pieces, rest = refs[1], refs[2:]
    else:
        pairs, pieces, rest = refs[1:5], refs[-1], refs[5:-1]
    gain, gain_own, key_row, weight = rest[:4]
    if stashed:
        out_values, out_probs, out_normed, out_centered, out_inv = rest[4:9]
    else:
        (out_mixed,) = rest[4:5]
    total, normed_own, mean_ref, inv_ref, weights, blocks, sems = rest[-7:]
    step = pl.program_id(0)
    full = width * PEERS
    heads = width // HEAD

    @pl.when(step == 0)
    def _():
        for k in range(PEERS):
            pltpu.make_async_copy(row_block(weight, idx[k]), blocks.at[k], sems.at[k]).start()
        if not natural:
            for k in range(RINGX):
                pieces[2 * k : 2 * k + 2] = pairs[k][...]
        sums = jnp.zeros((tokens, HEAD), F32)
        squares = jnp.zeros((tokens, HEAD), F32)
        for r in range(PEERS):
            for c in range(heads):
                x = pieces[r, :, c * HEAD : (c + 1) * HEAD].astype(F32)
                sums += x
                squares += x * x
        mean = jnp.sum(sums, -1, keepdims=True) / full
        variance = jnp.sum(squares, -1, keepdims=True) / full - mean * mean
        mean_ref[...] = jnp.broadcast_to(mean, (tokens, HEAD))
        inv_ref[...] = jnp.broadcast_to(lax.rsqrt(variance + EPSILON), (tokens, HEAD))
        total[...] = jnp.zeros_like(total)
        mine = (pieces[idx[PEERS]].astype(F32) - mean_ref[:, :1]) * inv_ref[:, :1]
        normed_own[...] = (mine * gain_own[0]).astype(BF16)
        keys = (normed_own[...].astype(F32) * key_row[...]).astype(BF16)
        probs = softmax_scores(normed_own[...], keys, tokens, heads)
        if stashed:
            out_probs[...] = probs
            out_normed[...] = normed_own[...]
        else:
            weights[...] = probs.astype(BF16)

    centered = (pieces[step].astype(F32) - mean_ref[:, :1]) * inv_ref[:, :1]
    normed = (centered * gain[0]).astype(BF16)
    wait_block(weight, blocks, sems, step, row_block)
    total[...] += lax.dot_general(normed, blocks[step], NN, preferred_element_type=F32)

    if stashed:
        share = tokens // PEERS
        for dz in range(2):
            rows = pl.ds(pl.multiple_of(idx[PEERS + 1 + dz] * share, share), share)
            out_centered[dz, 0] = (
                pieces[step, rows, :].astype(F32) - mean_ref[rows, :1]
            ) * inv_ref[rows, :1]
            out_inv[dz] = inv_ref[rows, :]

    @pl.when(step == PEERS - 1)
    def _():
        values = total[...].astype(BF16)
        if stashed:
            out_values[...] = values
        else:
            for h in range(heads):
                part = slice(h * HEAD, (h + 1) * HEAD)
                out_mixed[:, part] = lax.dot_general(
                    weights[h * tokens : (h + 1) * tokens],
                    values[:, part],
                    NN,
                    preferred_element_type=F32,
                ).astype(BF16)


def layer_call(stashed, idx, pieces, gain, key_row, weight):
    natural = len(pieces) == 1
    tokens, width = pieces[0].shape[-2:]
    full = width * PEERS
    share = tokens // PEERS
    heads = width // HEAD
    if stashed:
        out_shape = (
            jax.ShapeDtypeStruct((tokens, width), BF16),
            jax.ShapeDtypeStruct((heads * tokens, tokens), F32),
            jax.ShapeDtypeStruct((tokens, width), BF16),
            jax.ShapeDtypeStruct((2, PEERS, share, width), F32),
            jax.ShapeDtypeStruct((2, share, HEAD), F32),
        )
        out_specs = (
            pl.BlockSpec((tokens, width), lambda r, idx: (0, 0)),
            pl.BlockSpec((heads * tokens, tokens), lambda r, idx: (0, 0)),
            pl.BlockSpec((tokens, width), lambda r, idx: (0, 0)),
            pl.BlockSpec((2, 1, share, width), lambda r, idx: (0, idx[r], 0, 0)),
            pl.BlockSpec((2, share, HEAD), lambda r, idx: (0, 0, 0)),
        )
    else:
        out_shape = jax.ShapeDtypeStruct((tokens, width), BF16)
        out_specs = pl.BlockSpec((tokens, width), lambda r, idx: (0, 0))

    def body(*refs):
        layer_body(stashed, natural, tokens, width, *refs)

    scratch = [
        pltpu.VMEM((tokens, width), F32),
        pltpu.VMEM((tokens, width), BF16),
        pltpu.VMEM((tokens, HEAD), F32),
        pltpu.VMEM((tokens, HEAD), F32),
        pltpu.VMEM((heads * tokens, tokens), BF16),
    ] + stream_scratch(PEERS, width)
    if not natural:
        scratch.append(pltpu.VMEM((PEERS, tokens, width), BF16))
    return pl.pallas_call(
        body,
        out_shape=out_shape,
        grid_spec=pltpu.PrefetchScalarGridSpec(
            num_scalar_prefetch=1,
            grid=(PEERS,),
            in_specs=[whole(p) for p in pieces]
            + [
                pl.BlockSpec((1, 1, width), lambda r, idx: (idx[r], 0, 0)),
                pl.BlockSpec((1, 1, width), lambda r, idx: (idx[PEERS + 1], 0, 0)),
                whole(key_row),
                HBM,
            ],
            out_specs=out_specs,
            scratch_shapes=scratch,
        ),
        compiler_params=params(),
        cost_estimate=cost(2 * tokens * full * width, 2 * full * width),
        name="stash_layer" if stashed else "mix_layer",
    )(idx, *pieces, gain, gain, key_row, weight)


def project_call(idx, mixed, tiles):
    tokens, width = mixed.shape
    order = (4, 5, 2, 3, 6, 7, 0, 1)

    def body(idx, mixed, tiles, far, plus, minus, here, blocks, sems):
        copies = [
            pltpu.make_async_copy(column_block(tiles, idx[r]), blocks.at[k], sems.at[k])
            for k, r in enumerate(order)
        ]
        for each in copies:
            each.start()
        for k in range(len(order)):
            copies[k].wait()
            (far, plus, minus, here)[k // 2][k % 2] = lax.dot_general(
                mixed[...], blocks[k], NN, preferred_element_type=F32
            ).astype(BF16)

    pair = pl.BlockSpec((2, tokens, width), lambda r, idx: (0, 0, 0))
    return pl.pallas_call(
        body,
        out_shape=[jax.ShapeDtypeStruct((2, tokens, width), BF16)] * RINGX,
        grid_spec=pltpu.PrefetchScalarGridSpec(
            num_scalar_prefetch=1,
            grid=(1,),
            in_specs=[whole(mixed), HBM],
            out_specs=[pair] * RINGX,
            scratch_shapes=stream_scratch(PEERS, width),
        ),
        compiler_params=params(),
        cost_estimate=cost(16 * tokens * width * width, 16 * width * width),
        name="project",
    )(idx, mixed, tiles)


def sent_call(plan, place, held):
    _, tokens, width = held.shape
    steps = plan.shape[1]

    def body(plan, place, held, out):
        out[...] = held[...]

    def slot(t, plan, place):
        return plan[(place[0] * steps + t) * 2 + 1], 0, 0

    return pl.pallas_call(
        body,
        out_shape=jax.ShapeDtypeStruct((steps, tokens, width), BF16),
        grid_spec=pltpu.PrefetchScalarGridSpec(
            num_scalar_prefetch=2,
            grid=(steps,),
            in_specs=[pl.BlockSpec((1, tokens, width), slot)],
            out_specs=pl.BlockSpec((1, tokens, width), lambda t, plan, place: (t, 0, 0)),
        ),
        compiler_params=params(),
        cost_estimate=cost(1, 1),
        name="sent_blocks",
    )(plan.reshape(-1), place, held)


def chosen_call(plan, place, held, got, first):
    count, tokens, width = got.shape
    steps = plan.shape[1]

    def body(plan, place, held, got, out):
        side = plan[(place[1] * steps + first + pl.program_id(0)) * 2]

        @pl.when(side == 0)
        def _():
            out[...] = held[...]

        @pl.when(side != 0)
        def _():
            out[...] = got[...]

    def slot(t, plan, place):
        return plan[(place[1] * steps + first + t) * 2 + 1], 0, 0

    block = pl.BlockSpec((1, tokens, width), lambda t, plan, place: (t, 0, 0))
    return pl.pallas_call(
        body,
        out_shape=jax.ShapeDtypeStruct(got.shape, BF16),
        grid_spec=pltpu.PrefetchScalarGridSpec(
            num_scalar_prefetch=2,
            grid=(count,),
            in_specs=[pl.BlockSpec((1, tokens, width), slot), block],
            out_specs=block,
        ),
        compiler_params=params(),
        cost_estimate=cost(1, 1),
        name="chosen_blocks",
    )(plan.reshape(-1), place, held, got)


def attention_grad_call(idx, pieces, stashed, key_row, weight):
    share, width = pieces[0].shape[-2:]
    tokens = share * PEERS
    full = width * PEERS
    values, probs, normed = stashed

    def body(
        idx, pair, plus, far, minus, values, probs, normed, key_row,
        weight, out_values, out_direct, grads, total, sort_values, sort_direct, blocks, sems,
    ):
        step = pl.program_id(0)
        heads = width // HEAD

        def rows(r):
            return pl.ds(pl.multiple_of(idx[r] * share, share), share)

        @pl.when(step == 0)
        def _():
            for k in range(PEERS):
                pltpu.make_async_copy(
                    column_block(weight, k), blocks.at[k], sems.at[k]
                ).start()
            for k, part in enumerate((pair, plus, far, minus)):
                for dz in range(2):
                    for c in range(PEERS):
                        grads[c, rows(2 * k + dz)] = part[dz, c]
            total[...] = jnp.zeros_like(total)

        wait_block(weight, blocks, sems, step, column_block)
        total[...] += lax.dot_general(
            grads[step], blocks[step], NT, preferred_element_type=F32
        )

        @pl.when(step == PEERS - 1)
        def _():
            grad_mixed = total[...].astype(BF16)
            grad_probs = per_head(
                heads,
                lambda p: lax.dot_general(
                    grad_mixed[:, p], values[:, p], NT, preferred_element_type=F32
                ),
            )
            weights = probs[...]
            grad_scores = (
                weights
                * (grad_probs - jnp.sum(grad_probs * weights, -1, keepdims=True))
                / math.sqrt(HEAD)
            ).astype(BF16)
            weights = weights.astype(BF16)
            queries = normed[...]
            keys = (queries.astype(F32) * key_row[...]).astype(BF16)
            for h in range(heads):
                part = slice(h * HEAD, (h + 1) * HEAD)
                rows_of = slice(h * tokens, (h + 1) * tokens)
                grad_values = lax.dot_general(
                    weights[rows_of], grad_mixed[:, part], TN, preferred_element_type=F32
                )
                grad_query = lax.dot_general(
                    grad_scores[rows_of], keys[:, part], NN, preferred_element_type=F32
                )
                grad_keys = lax.dot_general(
                    grad_scores[rows_of], queries[:, part], TN, preferred_element_type=F32
                )
                sort_values[:, part] = grad_values.astype(BF16)
                sort_direct[:, part] = grad_query + grad_keys * key_row[:, part]
            for r in range(PEERS):
                out_values[r * share : (r + 1) * share] = sort_values[rows(r)]
                out_direct[r * share : (r + 1) * share] = sort_direct[rows(r)]

    result = pl.BlockSpec((tokens, width), lambda r, idx: (0, 0))
    return pl.pallas_call(
        body,
        out_shape=(
            jax.ShapeDtypeStruct((tokens, width), BF16),
            jax.ShapeDtypeStruct((tokens, width), F32),
        ),
        grid_spec=pltpu.PrefetchScalarGridSpec(
            num_scalar_prefetch=1,
            grid=(PEERS,),
            in_specs=[whole(p) for p in pieces]
            + [whole(values), whole(probs), whole(normed), whole(key_row)]
            + [HBM],
            out_specs=(result, result),
            scratch_shapes=[
                pltpu.VMEM((PEERS, tokens, width), BF16),
                pltpu.VMEM((tokens, width), F32),
                pltpu.VMEM((tokens, width), BF16),
                pltpu.VMEM((tokens, width), F32),
            ]
            + stream_scratch(PEERS, width),
        ),
        compiler_params=params(),
        cost_estimate=cost(2 * tokens * full * width, 2 * full * width),
        name="attention_grad",
    )(idx, *pieces, values, probs, normed, key_row, weight)


def back_project_call(idx, grad_values, direct, weight):
    tokens, width = grad_values.shape
    full = width * PEERS
    share = tokens // PEERS

    def body(
        idx, grad_values, direct, weight, here, plus, far, minus, blocks, sems
    ):
        step = pl.program_id(0)

        @pl.when(step == 0)
        def _():
            for k in range(PEERS):
                pltpu.make_async_copy(row_block(weight, k), blocks.at[k], sems.at[k]).start()

        wait_block(weight, blocks, sems, step, row_block)
        product = lax.dot_general(
            grad_values[...], blocks[step], NT, preferred_element_type=F32
        )
        mine = (step == idx[0]).astype(F32)
        product = (product + direct[...] * mine).astype(BF16)

        def piece(r):
            return product[r * share : (r + 1) * share]

        for k, part in enumerate((here, plus, far, minus)):
            for dz in range(2):
                part[dz, 0] = piece(2 * k + dz)

    return pl.pallas_call(
        body,
        out_shape=[jax.ShapeDtypeStruct((2, PEERS, share, width), BF16)] * RINGX,
        grid_spec=pltpu.PrefetchScalarGridSpec(
            num_scalar_prefetch=1,
            grid=(PEERS,),
            in_specs=[
                pl.BlockSpec((tokens, width), lambda c, idx: (0, 0)),
                pl.BlockSpec((tokens, width), lambda c, idx: (0, 0)),
                HBM,
            ],
            scratch_shapes=stream_scratch(PEERS, width),
            out_specs=[pl.BlockSpec((2, 1, share, width), lambda c, idx: (0, c, 0, 0))] * RINGX,
        ),
        compiler_params=params(),
        cost_estimate=cost(2 * tokens * full * width, 2 * full * width),
        name="back_project",
    )(idx, grad_values, direct, weight)


def norm_grad_call(parts, gain, centered, inv_std, grad_own):
    _, blocks, share, width = parts[0].shape
    full = blocks * width

    def body(*refs):
        parts, (gain, centered, inv_std, grad_own, out) = refs[:RINGX], refs[RINGX:]
        for dz in range(2):
            scaled = sum(part[dz].astype(F32) for part in parts) * gain[...]
            mid = centered[dz]
            first = jnp.sum(jnp.sum(scaled, 0), -1, keepdims=True) / full
            second = jnp.sum(jnp.sum(scaled * mid, 0), -1, keepdims=True) / full
            result = inv_std[dz][:, :1][None] * (scaled - first[None] - mid * second[None])
            if dz == 0:
                result = result + grad_own[...].astype(F32)
            out[dz] = result.astype(BF16)

    return pl.pallas_call(
        body,
        out_shape=jax.ShapeDtypeStruct(parts[0].shape, BF16),
        compiler_params=pltpu.CompilerParams(vmem_limit_bytes=VMEM_LIMIT),
        cost_estimate=cost(1, 1),
        name="norm_grad",
    )(*parts, gain, centered, inv_std, grad_own)


def swap_layout(array):
    return lax.all_to_all(array, "tp", split_axis=0, concat_axis=0, tiled=True)


def per_device(
    inputs, cotangents, carried, pending, stash, stash_plan, gain, key_gain, w_value, w_out
):
    steps = inputs.shape[0] + 1
    tokens = carried.shape[1]
    width = key_gain.shape[-1]
    share = tokens // PEERS
    me = lax.axis_index("tp")
    places = [place(me, r // 2, r % 2) for r in range(PEERS)]
    relative = jnp.stack(places + [jnp.zeros_like(me), me, me ^ 1]).astype(jnp.int32)
    natural = jnp.stack(
        [jnp.full_like(me, r) for r in range(PEERS)] + [me, me, me ^ 1]
    ).astype(jnp.int32)
    section = lax.axis_index("section")
    sections = lax.axis_size("section")
    mirror = sections - 1 - section
    gain_blocks = gain[0].reshape(PEERS, 1, width)
    held = stash[0]
    place_of = jnp.stack([mirror, section]).astype(jnp.int32)

    order = Order()
    pin = order.pin

    def from_mirror(array):
        return lax.ppermute(array, "section", [(i, sections - 1 - i) for i in range(sections)])

    def finished(parts):
        own = jnp.stack([p[0] for p in parts])
        return own, shift(pin(jnp.stack([p[1] for p in parts])), 0, 1)

    def mix(pieces):
        mixed = pin(layer_call(False, relative, pin(*pieces), gain_blocks, key_gain, tiles))
        far, plus, minus, here = pin(*project_call(relative, mixed, tiles))
        return ScatterSum(order, far, plus, minus), here

    def stash_layer(idx, pieces):
        pieces = pin(*pieces)
        pieces = pieces if isinstance(pieces, list) else [pieces]
        return pin(*layer_call(True, idx, pieces, gain_blocks, key_gain, tiles))

    is_first = section == 0
    is_last = section == sections - 1
    residual_place = (jnp.arange(2) == 0).astype(F32)[:, None, None]

    own = pin(carried[0])
    partner = shift(own, 0, 1)
    sent = pin(sent_call(stash_plan, place_of, held))
    mirrored = from_mirror(pin(sent[:1]))
    spread = swap_layout(
        pin(
            jnp.concatenate([pending, cotangents])
            .reshape(steps, PEERS, share, width)
            .transpose(1, 0, 2, 3)
        )
    )
    fwd_pair = jnp.stack([own, pin(partner)])
    fwd_gather = Gather(order, fwd_pair)
    stash_own = pin(chosen_call(stash_plan, place_of, held, pin(mirrored), 0))[0]
    stash_partner = shift(stash_own, 0, 1)
    tiles = pin(tile_call(*pin(w_value[0], w_out[0])))
    stash_gather = Gather(order, jnp.stack([stash_own, pin(stash_partner)]))
    spread = pin(spread).transpose(1, 0, 2, 3)
    grad_own = pin(spread[0])
    grad_partner = shift(grad_own, 0, 1)
    fwd_sums, here = mix(fwd_gather.done())
    grad_pair = jnp.stack([grad_own, pin(grad_partner)])
    grad_gather = Gather(order, grad_pair)
    late = from_mirror(pin(sent[1:]))

    forward_parts = []
    backward_parts = []
    grad_sums = None
    for t in range(steps):
        if t > 0:
            backward_parts.append(
                pin(
                    norm_grad_call(
                        (here_grad, *grad_sums.done()),
                        gain_blocks,
                        centered,
                        inv_std,
                        grad_pair[0],
                    )
                )
            )
            grad_hop = Hop(order, backward_parts[-1], -1)
            stashed = stash_layer(natural, (stash_later[t - 1],))
        else:
            stashed = stash_layer(relative, stash_gather.done())
            input_pairs = jnp.stack([inputs, partner_in(pin(inputs), 0)], 1)
            cotangent_pairs = jnp.stack(
                [spread[1:], partner_in(pin(spread[1:]), sections - 1)], 1
            )
        forward_parts.append(
            (
                sum(part.astype(F32) for part in (here, *fwd_sums.done()))
                + fwd_pair[:1].astype(F32) * residual_place
            ).astype(BF16)
        )
        if t + 1 < steps:
            fwd_hop = Hop(order, forward_parts[-1], 1)
        else:
            forward_last = finished(forward_parts[-1:])
        if t > 0:
            grad_pair = grad_hop.done(is_last, cotangent_pairs[t - 1])
            grad_gather = Gather(order, grad_pair)
        else:
            late = pin(chosen_call(stash_plan, place_of, held, pin(late), 1))
            stash_later = [
                lax.all_gather(late[k], "tp", axis=0) for k in range(steps - 1)
            ]
        if t + 1 < steps:
            fwd_pair = fwd_hop.done(is_first, input_pairs[t])
            fwd_gather = Gather(order, fwd_pair)
        else:
            forward_early = finished(forward_parts[:-1])
            backward_early = finished(backward_parts)
        values, probs, normed, centered, inv_std = stashed
        grad_values, direct = pin(
            *attention_grad_call(
                relative, grad_gather.done(), (values, probs, normed), key_gain, tiles
            )
        )
        here_grad, plus, far, minus = pin(
            *back_project_call(relative, grad_values, direct, tiles)
        )
        grad_sums = ScatterSum(order, far, plus, minus)
        if t + 1 < steps:
            fwd_sums, here = mix(fwd_gather.done())

    early = add(*pin(*backward_early)).transpose(1, 0, 2, 3)
    early = swap_layout(pin(early))
    last_part = norm_grad_call(
        (here_grad, *grad_sums.done()), gain_blocks, centered, inv_std, grad_pair[0]
    )
    backward_last = finished([last_part])
    forward = jnp.concatenate([add(*forward_early), add(*forward_last)])
    last = swap_layout(add(*backward_last)[0])[None]
    backward = jnp.concatenate([early.transpose(1, 0, 2, 3), last])
    return (forward[None], backward.reshape(1, steps, tokens, width))


def solution(mesh):
    return jax.shard_map(
        per_device,
        mesh=mesh,
        in_specs=(
            P(None, None, "tp"),
            P(None, None, "tp"),
            P("section", None, "tp"),
            P("section", None, "tp"),
            P("section", None, None, "tp"),
            P(),
            P("section", None),
            P("section", "tp"),
            P("section", None, "tp"),
            P("section", "tp", None),
        ),
        out_specs=(P("section", None, None, "tp"), P("section", None, None, "tp")),
        check_vma=False,
    )
```

```python
import math

import jax
import jax.numpy as jnp
from jax import lax
from jax.experimental import pallas as pl
from jax.experimental.pallas import tpu as pltpu
from jax.sharding import PartitionSpec as P

HEAD = 128
EPSILON = 1e-05
RINGX = 4
PEERS = 8
BF16 = jnp.bfloat16
VMEM_LIMIT = 46 * 1024 * 1024
F32 = jnp.float32
HBM = pl.BlockSpec(memory_space=pl.ANY)
NT = (((1,), (1,)), ((), ()))
NN = (((1,), (0,)), ((), ()))
TN = (((0,), (0,)), ((), ()))


def params():
    return pltpu.CompilerParams(
        dimension_semantics=("arbitrary",), vmem_limit_bytes=VMEM_LIMIT
    )


def cost(flops, nbytes):
    return pl.CostEstimate(flops=1, bytes_accessed=1, transcendentals=0)


def place(i, dx, dz):
    return ((i // 2 + dx) % RINGX) * 2 + ((i % 2) ^ dz)


def shift(array, dx, dz):
    return lax.ppermute(array, "tp", [(i, place(i, dx, dz)) for i in range(PEERS)])


def hop(array, by, cross):
    peers = lax.axis_size("section")
    pairs = [
        (i * PEERS + j, (i + by) * PEERS + (j ^ cross))
        for i in range(peers)
        if 0 <= i + by < peers
        for j in range(PEERS)
    ]
    return lax.ppermute(array, ("section", "tp"), pairs)


def partner_in(array, section):
    pairs = [(section * PEERS + j, section * PEERS + (j ^ 1)) for j in range(PEERS)]
    return lax.ppermute(array, ("section", "tp"), pairs)


def add(a, b):
    return (a.astype(F32) + b.astype(F32)).astype(BF16)


class Order:
    def __init__(self):
        self.token = jnp.zeros((), F32)

    def pin(self, *arrays):
        self.token, *arrays = lax.optimization_barrier((self.token, *arrays))
        return arrays if len(arrays) > 1 else arrays[0]


class Gather:
    def __init__(self, order, pair):
        self.order = order
        self.pair = order.pin(pair)
        far = shift(self.pair, 2, 0)
        self.rest = shift(self.pair, -1, 0), far, shift(self.pair, 1, 0)

    def done(self):
        return self.pair, *self.order.pin(*self.rest)


class GatherQuads:
    def __init__(self, order, own):
        self.order = order
        own = order.pin(own)
        far = shift(own, 2, 0)
        self.got = own, shift(own, -1, 0), far, shift(own, 1, 0)

    def second(self):
        self.quad = jnp.stack(self.order.pin(*self.got))
        self.other = shift(self.quad, 0, 1)

    def done(self):
        return self.quad, self.order.pin(self.other)


class ScatterSum:
    def __init__(self, order, far, plus, minus):
        self.order = order
        far, plus, minus = order.pin(far, plus, minus)
        self.got = shift(far, 2, 0), shift(plus, 1, 0), shift(minus, -1, 0)

    def done(self):
        return self.order.pin(*self.got)


class Hop:
    def __init__(self, order, part, by):
        self.order = order
        part = order.pin(part)
        self.got = hop(part, by, 0), hop(part, by, 1)

    def done(self, at_edge, edge_pair):
        same, cross = self.order.pin(*self.got)
        return jnp.where(at_edge, edge_pair, add(same, cross[::-1]))


def whole(array):
    zeros = (0,) * array.ndim
    return pl.BlockSpec(array.shape, lambda r, idx: zeros)


def per_head(heads, product):
    return jnp.concatenate([product(slice(h * HEAD, (h + 1) * HEAD)) for h in range(heads)], 0)


def softmax_scores(queries, keys, tokens, heads):
    scores = per_head(
        heads,
        lambda p: lax.dot_general(queries[:, p], keys[:, p], NT, preferred_element_type=F32),
    )
    scores = scores / math.sqrt(HEAD)
    rows = lax.broadcasted_iota(jnp.int32, scores.shape, 0) % tokens
    columns = lax.broadcasted_iota(jnp.int32, scores.shape, 1)
    scores = jnp.where(columns <= rows, scores, -1e30)
    raised = jnp.exp(scores - jnp.max(scores, -1, keepdims=True))
    return raised / jnp.sum(raised, -1, keepdims=True)


def row_block(tiles, k):
    return tiles.at[k]


def column_block(tiles, k):
    return tiles.at[PEERS + k]


def tile_call(w_value, w_out):
    width = w_value.shape[1]

    def body(w_value, w_out, tiles):
        tiles[0, 0] = w_value[...]
        tiles[1, 0] = w_out[...]

    tiles = pl.pallas_call(
        body,
        out_shape=jax.ShapeDtypeStruct((2, PEERS, width, width), BF16),
        grid=(PEERS,),
        in_specs=[
            pl.BlockSpec((width, width), lambda k: (k, 0)),
            pl.BlockSpec((width, width), lambda k: (0, k)),
        ],
        out_specs=pl.BlockSpec((2, 1, width, width), lambda k: (0, k, 0, 0)),
        compiler_params=params(),
        cost_estimate=cost(1, 1),
        name="weight_tiles",
    )(w_value, w_out)
    return tiles.reshape(2 * PEERS, width, width)


def stream_scratch(count, width):
    return [pltpu.VMEM((count, width, width), BF16), pltpu.SemaphoreType.DMA((count,))]


def wait_block(weight, blocks, sems, step, block_of):
    pltpu.make_async_copy(block_of(weight, 0), blocks.at[step], sems.at[step]).wait()


def layer_body(stashed, count, tokens, width, *refs):
    idx = refs[0]
    parts, pieces, rest = refs[1 : 1 + count], refs[-1], refs[1 + count : -1]
    gain, gain_own, key_row, weight = rest[:4]
    if stashed:
        out_values, out_probs, out_normed, out_centered, out_inv = rest[4:9]
    else:
        (out_mixed,) = rest[4:5]
    total, normed_own, mean_ref, inv_ref, weights, blocks, sems = rest[-7:]
    step = pl.program_id(0)
    full = width * PEERS
    heads = width // HEAD

    @pl.when(step == 0)
    def _():
        for k in range(PEERS):
            pltpu.make_async_copy(row_block(weight, idx[k]), blocks.at[k], sems.at[k]).start()
        for k in range(PEERS):
            pieces[k] = parts[k // 2][k % 2] if count == RINGX else parts[k % 2][k // 2]
        sums = jnp.zeros((tokens, HEAD), F32)
        squares = jnp.zeros((tokens, HEAD), F32)
        for r in range(PEERS):
            for c in range(heads):
                x = pieces[r, :, c * HEAD : (c + 1) * HEAD].astype(F32)
                sums += x
                squares += x * x
        mean = jnp.sum(sums, -1, keepdims=True) / full
        variance = jnp.sum(squares, -1, keepdims=True) / full - mean * mean
        mean_ref[...] = jnp.broadcast_to(mean, (tokens, HEAD))
        inv_ref[...] = jnp.broadcast_to(lax.rsqrt(variance + EPSILON), (tokens, HEAD))
        total[...] = jnp.zeros_like(total)
        mine = (pieces[idx[PEERS]].astype(F32) - mean_ref[:, :1]) * inv_ref[:, :1]
        normed_own[...] = (mine * gain_own[0]).astype(BF16)
        keys = (normed_own[...].astype(F32) * key_row[...]).astype(BF16)
        probs = softmax_scores(normed_own[...], keys, tokens, heads)
        if stashed:
            out_probs[...] = probs
            out_normed[...] = normed_own[...]
        else:
            weights[...] = probs.astype(BF16)

    centered = (pieces[step].astype(F32) - mean_ref[:, :1]) * inv_ref[:, :1]
    normed = (centered * gain[0]).astype(BF16)
    wait_block(weight, blocks, sems, step, row_block)
    total[...] += lax.dot_general(normed, blocks[step], NN, preferred_element_type=F32)

    if stashed:
        share = tokens // PEERS
        for dz in range(2):
            rows = pl.ds(pl.multiple_of(idx[PEERS + 1 + dz] * share, share), share)
            out_centered[dz, 0] = (
                pieces[step, rows, :].astype(F32) - mean_ref[rows, :1]
            ) * inv_ref[rows, :1]
            out_inv[dz] = inv_ref[rows, :]

    @pl.when(step == PEERS - 1)
    def _():
        values = total[...].astype(BF16)
        if stashed:
            out_values[...] = values
        else:
            for h in range(heads):
                part = slice(h * HEAD, (h + 1) * HEAD)
                out_mixed[:, part] = lax.dot_general(
                    weights[h * tokens : (h + 1) * tokens],
                    values[:, part],
                    NN,
                    preferred_element_type=F32,
                ).astype(BF16)


def layer_call(stashed, idx, pieces, gain, key_row, weight):
    count = len(pieces)
    tokens, width = pieces[0].shape[-2:]
    full = width * PEERS
    share = tokens // PEERS
    heads = width // HEAD
    if stashed:
        out_shape = (
            jax.ShapeDtypeStruct((tokens, width), BF16),
            jax.ShapeDtypeStruct((heads * tokens, tokens), F32),
            jax.ShapeDtypeStruct((tokens, width), BF16),
            jax.ShapeDtypeStruct((2, PEERS, share, width), F32),
            jax.ShapeDtypeStruct((2, share, HEAD), F32),
        )
        out_specs = (
            pl.BlockSpec((tokens, width), lambda r, idx: (0, 0)),
            pl.BlockSpec((heads * tokens, tokens), lambda r, idx: (0, 0)),
            pl.BlockSpec((tokens, width), lambda r, idx: (0, 0)),
            pl.BlockSpec((2, 1, share, width), lambda r, idx: (0, idx[r], 0, 0)),
            pl.BlockSpec((2, share, HEAD), lambda r, idx: (0, 0, 0)),
        )
    else:
        out_shape = jax.ShapeDtypeStruct((tokens, width), BF16)
        out_specs = pl.BlockSpec((tokens, width), lambda r, idx: (0, 0))

    def body(*refs):
        layer_body(stashed, count, tokens, width, *refs)

    scratch = [
        pltpu.VMEM((tokens, width), F32),
        pltpu.VMEM((tokens, width), BF16),
        pltpu.VMEM((tokens, HEAD), F32),
        pltpu.VMEM((tokens, HEAD), F32),
        pltpu.VMEM((heads * tokens, tokens), BF16),
    ] + stream_scratch(PEERS, width)
    scratch.append(pltpu.VMEM((PEERS, tokens, width), BF16))
    return pl.pallas_call(
        body,
        out_shape=out_shape,
        grid_spec=pltpu.PrefetchScalarGridSpec(
            num_scalar_prefetch=1,
            grid=(PEERS,),
            in_specs=[whole(p) for p in pieces]
            + [
                pl.BlockSpec((1, 1, width), lambda r, idx: (idx[r], 0, 0)),
                pl.BlockSpec((1, 1, width), lambda r, idx: (idx[PEERS + 1], 0, 0)),
                whole(key_row),
                HBM,
            ],
            out_specs=out_specs,
            scratch_shapes=scratch,
        ),
        compiler_params=params(),
        cost_estimate=cost(2 * tokens * full * width, 2 * full * width),
        name="stash_layer" if stashed else "mix_layer",
    )(idx, *pieces, gain, gain, key_row, weight)


def project_call(idx, mixed, tiles):
    tokens, width = mixed.shape
    order = (4, 5, 2, 3, 6, 7, 0, 1)

    def body(idx, mixed, tiles, far, plus, minus, here, blocks, sems):
        copies = [
            pltpu.make_async_copy(column_block(tiles, idx[r]), blocks.at[k], sems.at[k])
            for k, r in enumerate(order)
        ]
        for each in copies:
            each.start()
        for k in range(len(order)):
            copies[k].wait()
            (far, plus, minus, here)[k // 2][k % 2] = lax.dot_general(
                mixed[...], blocks[k], NN, preferred_element_type=F32
            ).astype(BF16)

    pair = pl.BlockSpec((2, tokens, width), lambda r, idx: (0, 0, 0))
    return pl.pallas_call(
        body,
        out_shape=[jax.ShapeDtypeStruct((2, tokens, width), BF16)] * RINGX,
        grid_spec=pltpu.PrefetchScalarGridSpec(
            num_scalar_prefetch=1,
            grid=(1,),
            in_specs=[whole(mixed), HBM],
            out_specs=[pair] * RINGX,
            scratch_shapes=stream_scratch(PEERS, width),
        ),
        compiler_params=params(),
        cost_estimate=cost(16 * tokens * width * width, 16 * width * width),
        name="project",
    )(idx, mixed, tiles)


def sent_call(plan, place, held):
    _, tokens, width = held.shape
    steps = plan.shape[1]

    def body(plan, place, held, out):
        out[...] = held[...]

    def slot(t, plan, place):
        return plan[(place[0] * steps + t) * 2 + 1], 0, 0

    return pl.pallas_call(
        body,
        out_shape=jax.ShapeDtypeStruct((steps, tokens, width), BF16),
        grid_spec=pltpu.PrefetchScalarGridSpec(
            num_scalar_prefetch=2,
            grid=(steps,),
            in_specs=[pl.BlockSpec((1, tokens, width), slot)],
            out_specs=pl.BlockSpec((1, tokens, width), lambda t, plan, place: (t, 0, 0)),
        ),
        compiler_params=params(),
        cost_estimate=cost(1, 1),
        name="sent_blocks",
    )(plan.reshape(-1), place, held)


def chosen_call(plan, place, held, got, first):
    count, tokens, width = got.shape
    steps = plan.shape[1]

    def body(plan, place, held, got, out):
        side = plan[(place[1] * steps + first + pl.program_id(0)) * 2]

        @pl.when(side == 0)
        def _():
            out[...] = held[...]

        @pl.when(side != 0)
        def _():
            out[...] = got[...]

    def slot(t, plan, place):
        return plan[(place[1] * steps + first + t) * 2 + 1], 0, 0

    block = pl.BlockSpec((1, tokens, width), lambda t, plan, place: (t, 0, 0))
    return pl.pallas_call(
        body,
        out_shape=jax.ShapeDtypeStruct(got.shape, BF16),
        grid_spec=pltpu.PrefetchScalarGridSpec(
            num_scalar_prefetch=2,
            grid=(count,),
            in_specs=[pl.BlockSpec((1, tokens, width), slot), block],
            out_specs=block,
        ),
        compiler_params=params(),
        cost_estimate=cost(1, 1),
        name="chosen_blocks",
    )(plan.reshape(-1), place, held, got)


def attention_grad_call(idx, pieces, stashed, key_row, weight):
    share, width = pieces[0].shape[-2:]
    tokens = share * PEERS
    full = width * PEERS
    values, probs, normed = stashed

    def body(
        idx, pair, plus, far, minus, values, probs, normed, key_row,
        weight, out_values, out_direct, grads, total, sort_values, sort_direct, blocks, sems,
    ):
        step = pl.program_id(0)
        heads = width // HEAD

        def rows(r):
            return pl.ds(pl.multiple_of(idx[r] * share, share), share)

        @pl.when(step == 0)
        def _():
            for k in range(PEERS):
                pltpu.make_async_copy(
                    column_block(weight, k), blocks.at[k], sems.at[k]
                ).start()
            for k, part in enumerate((pair, plus, far, minus)):
                for dz in range(2):
                    for c in range(PEERS):
                        grads[c, rows(2 * k + dz)] = part[dz, c]
            total[...] = jnp.zeros_like(total)

        wait_block(weight, blocks, sems, step, column_block)
        total[...] += lax.dot_general(
            grads[step], blocks[step], NT, preferred_element_type=F32
        )

        @pl.when(step == PEERS - 1)
        def _():
            grad_mixed = total[...].astype(BF16)
            grad_probs = per_head(
                heads,
                lambda p: lax.dot_general(
                    grad_mixed[:, p], values[:, p], NT, preferred_element_type=F32
                ),
            )
            weights = probs[...]
            grad_scores = (
                weights
                * (grad_probs - jnp.sum(grad_probs * weights, -1, keepdims=True))
                / math.sqrt(HEAD)
            ).astype(BF16)
            weights = weights.astype(BF16)
            queries = normed[...]
            keys = (queries.astype(F32) * key_row[...]).astype(BF16)
            for h in range(heads):
                part = slice(h * HEAD, (h + 1) * HEAD)
                rows_of = slice(h * tokens, (h + 1) * tokens)
                grad_values = lax.dot_general(
                    weights[rows_of], grad_mixed[:, part], TN, preferred_element_type=F32
                )
                grad_query = lax.dot_general(
                    grad_scores[rows_of], keys[:, part], NN, preferred_element_type=F32
                )
                grad_keys = lax.dot_general(
                    grad_scores[rows_of], queries[:, part], TN, preferred_element_type=F32
                )
                sort_values[:, part] = grad_values.astype(BF16)
                sort_direct[:, part] = grad_query + grad_keys * key_row[:, part]
            for r in range(PEERS):
                out_values[r * share : (r + 1) * share] = sort_values[rows(r)]
                out_direct[r * share : (r + 1) * share] = sort_direct[rows(r)]

    result = pl.BlockSpec((tokens, width), lambda r, idx: (0, 0))
    return pl.pallas_call(
        body,
        out_shape=(
            jax.ShapeDtypeStruct((tokens, width), BF16),
            jax.ShapeDtypeStruct((tokens, width), F32),
        ),
        grid_spec=pltpu.PrefetchScalarGridSpec(
            num_scalar_prefetch=1,
            grid=(PEERS,),
            in_specs=[whole(p) for p in pieces]
            + [whole(values), whole(probs), whole(normed), whole(key_row)]
            + [HBM],
            out_specs=(result, result),
            scratch_shapes=[
                pltpu.VMEM((PEERS, tokens, width), BF16),
                pltpu.VMEM((tokens, width), F32),
                pltpu.VMEM((tokens, width), BF16),
                pltpu.VMEM((tokens, width), F32),
            ]
            + stream_scratch(PEERS, width),
        ),
        compiler_params=params(),
        cost_estimate=cost(2 * tokens * full * width, 2 * full * width),
        name="attention_grad",
    )(idx, *pieces, values, probs, normed, key_row, weight)


def back_project_call(idx, grad_values, direct, weight):
    tokens, width = grad_values.shape
    full = width * PEERS
    share = tokens // PEERS

    def body(
        idx, grad_values, direct, weight, here, plus, far, minus, blocks, sems
    ):
        step = pl.program_id(0)

        @pl.when(step == 0)
        def _():
            for k in range(PEERS):
                pltpu.make_async_copy(row_block(weight, k), blocks.at[k], sems.at[k]).start()

        wait_block(weight, blocks, sems, step, row_block)
        product = lax.dot_general(
            grad_values[...], blocks[step], NT, preferred_element_type=F32
        )
        mine = (step == idx[0]).astype(F32)
        product = (product + direct[...] * mine).astype(BF16)

        def piece(r):
            return product[r * share : (r + 1) * share]

        for k, part in enumerate((here, plus, far, minus)):
            for dz in range(2):
                part[dz, 0] = piece(2 * k + dz)

    return pl.pallas_call(
        body,
        out_shape=[jax.ShapeDtypeStruct((2, PEERS, share, width), BF16)] * RINGX,
        grid_spec=pltpu.PrefetchScalarGridSpec(
            num_scalar_prefetch=1,
            grid=(PEERS,),
            in_specs=[
                pl.BlockSpec((tokens, width), lambda c, idx: (0, 0)),
                pl.BlockSpec((tokens, width), lambda c, idx: (0, 0)),
                HBM,
            ],
            scratch_shapes=stream_scratch(PEERS, width),
            out_specs=[pl.BlockSpec((2, 1, share, width), lambda c, idx: (0, c, 0, 0))] * RINGX,
        ),
        compiler_params=params(),
        cost_estimate=cost(2 * tokens * full * width, 2 * full * width),
        name="back_project",
    )(idx, grad_values, direct, weight)


def norm_grad_call(parts, gain, centered, inv_std, grad_own, last=False):
    _, blocks, share, width = parts[0].shape
    full = blocks * width

    def body(*refs):
        parts, (gain, centered, inv_std, grad_own, out) = refs[:RINGX], refs[RINGX:]
        for dz in range(2):
            scaled = sum(part[dz].astype(F32) for part in parts) * gain[...]
            mid = centered[dz]
            first = jnp.sum(jnp.sum(scaled, 0), -1, keepdims=True) / full
            second = jnp.sum(jnp.sum(scaled * mid, 0), -1, keepdims=True) / full
            result = inv_std[dz][:, :1][None] * (scaled - first[None] - mid * second[None])
            if dz == 0:
                result = result + grad_own[...].astype(F32)
            if last:
                out[:, dz] = result.astype(BF16)
            else:
                out[dz] = result.astype(BF16)

    shape = (blocks, 2, share, width) if last else parts[0].shape
    return pl.pallas_call(
        body,
        out_shape=jax.ShapeDtypeStruct(shape, BF16),
        compiler_params=pltpu.CompilerParams(vmem_limit_bytes=VMEM_LIMIT),
        cost_estimate=cost(1, 1),
        name="norm_grad",
    )(*parts, gain, centered, inv_std, grad_own)


def swap_layout(array):
    return lax.all_to_all(array, "tp", split_axis=0, concat_axis=0, tiled=True)


def per_device(
    inputs, cotangents, carried, pending, stash, stash_plan, gain, key_gain, w_value, w_out
):
    steps = inputs.shape[0] + 1
    tokens = carried.shape[1]
    width = key_gain.shape[-1]
    share = tokens // PEERS
    me = lax.axis_index("tp")
    places = [place(me, r // 2, r % 2) for r in range(PEERS)]
    relative = jnp.stack(places + [jnp.zeros_like(me), me, me ^ 1]).astype(jnp.int32)
    section = lax.axis_index("section")
    sections = lax.axis_size("section")
    mirror = sections - 1 - section
    gain_blocks = gain[0].reshape(PEERS, 1, width)
    held = stash[0]
    place_of = jnp.stack([mirror, section]).astype(jnp.int32)

    order = Order()
    pin = order.pin

    def from_mirror(array):
        return lax.ppermute(array, "section", [(i, sections - 1 - i) for i in range(sections)])

    def finished(parts):
        own = jnp.stack([p[0] for p in parts])
        return own, shift(pin(jnp.stack([p[1] for p in parts])), 0, 1)

    def mix(pieces):
        mixed = pin(layer_call(False, relative, pin(*pieces), gain_blocks, key_gain, tiles))
        far, plus, minus, here = pin(*project_call(relative, mixed, tiles))
        return ScatterSum(order, far, plus, minus), here

    def stash_layer(idx, pieces):
        pieces = pin(*pieces)
        pieces = pieces if isinstance(pieces, list) else [pieces]
        return pin(*layer_call(True, idx, pieces, gain_blocks, key_gain, tiles))

    is_first = section == 0
    is_last = section == sections - 1
    residual_place = (jnp.arange(2) == 0).astype(F32)[:, None, None]

    spread = swap_layout(
        pin(
            jnp.concatenate([pending, cotangents])
            .reshape(steps, PEERS, share, width)
            .transpose(1, 0, 2, 3)
        )
    )
    own = pin(carried[0])
    partner = shift(own, 0, 1)
    sent = pin(sent_call(stash_plan, place_of, held))
    mirrored = from_mirror(sent[:1])
    tiles = pin(tile_call(*pin(w_value[0], w_out[0])))
    fwd_pair = jnp.stack([own, pin(partner)])
    fwd_gather = Gather(order, fwd_pair)
    stash_own = pin(chosen_call(stash_plan, place_of, held, pin(mirrored), 0))[0]
    stash_partner = shift(stash_own, 0, 1)
    spread = pin(spread).transpose(1, 0, 2, 3)
    grad_own = pin(spread[0])
    grad_partner = shift(grad_own, 0, 1)
    stash_gather = Gather(order, jnp.stack([stash_own, pin(stash_partner)]))
    fwd_sums, here = mix(fwd_gather.done())
    grad_pair = jnp.stack([grad_own, pin(grad_partner)])
    grad_gather = Gather(order, grad_pair)
    late = from_mirror(pin(sent[1:]))

    forward_parts = []
    backward_parts = []
    for t in range(steps):
        if t > 0:
            backward_parts.append(
                pin(
                    norm_grad_call(
                        (here_grad, *grad_sums.done()),
                        gain_blocks,
                        centered,
                        inv_std,
                        grad_pair[0],
                    )
                )
            )
            grad_hop = Hop(order, backward_parts[-1], -1)
        else:
            stashed = stash_layer(relative, stash_gather.done())
            grad_pieces = grad_gather.done()
        forward_parts.append(
            (
                sum(part.astype(F32) for part in (here, *fwd_sums.done()))
                + fwd_pair[:1].astype(F32) * residual_place
            ).astype(BF16)
        )
        if t + 1 < steps:
            fwd_hop = Hop(order, forward_parts[-1], 1)
        else:
            forward_last = finished(forward_parts[-1:])
        if t > 0:
            stashed = stash_layer(relative, stash_gather.done())
            grad_pair = grad_hop.done(is_last, cotangent_pairs[t - 1])
            grad_gather = Gather(order, grad_pair)
        else:
            late = pin(chosen_call(stash_plan, place_of, held, pin(late), 1))
            input_pairs = jnp.stack([inputs, partner_in(pin(inputs), 0)], 1)
            cotangent_pairs = jnp.stack(
                [spread[1:], partner_in(pin(spread[1:]), sections - 1)], 1
            )
        if t + 1 == steps:
            forward_early = finished(forward_parts[:-1])
            backward_early = finished(backward_parts)
        if t > 0:
            grad_pieces = grad_gather.done()
        values, probs, normed, centered, inv_std = stashed
        grad_values, direct = pin(
            *attention_grad_call(
                relative, grad_pieces, (values, probs, normed), key_gain, tiles
            )
        )
        if t + 1 < steps:
            fwd_pair = fwd_hop.done(is_first, input_pairs[t])
            fwd_gather = Gather(order, fwd_pair)
        here_grad, plus, far, minus = pin(
            *back_project_call(relative, *pin(grad_values, direct), tiles)
        )
        if t + 1 < steps:
            stash_gather = GatherQuads(order, late[t])
        grad_sums = ScatterSum(order, far, plus, minus)
        if t + 1 < steps:
            pieces = fwd_gather.done()
            fwd_sums, here = mix(pieces)
            stash_gather.second()

    early = add(*pin(*backward_early)).transpose(1, 0, 2, 3)
    early = swap_layout(pin(early))
    last_part = norm_grad_call(
        (here_grad, *grad_sums.done()), gain_blocks, centered, inv_std, grad_pair[0], True
    )
    last = swap_layout(last_part).reshape(RINGX, 2, 2, share, width)
    last = add(last[:, :, 0], last[:, ::-1, 1]).reshape(1, PEERS, share, width)
    forward = jnp.concatenate([add(*forward_early), add(*forward_last)])
    backward = jnp.concatenate([early.transpose(1, 0, 2, 3), last])
    return (forward[None], backward.reshape(1, steps, tokens, width))


def solution(mesh):
    return jax.shard_map(
        per_device,
        mesh=mesh,
        in_specs=(
            P(None, None, "tp"),
            P(None, None, "tp"),
            P("section", None, "tp"),
            P("section", None, "tp"),
            P("section", None, None, "tp"),
            P(),
            P("section", None),
            P("section", "tp"),
            P("section", None, "tp"),
            P("section", "tp", None),
        ),
        out_specs=(P("section", None, None, "tp"), P("section", None, None, "tp")),
        check_vma=False,
    )
```

```python
import math

import jax
import jax.numpy as jnp
from jax import lax
from jax.experimental import pallas as pl
from jax.experimental.pallas import tpu as pltpu
from jax.sharding import PartitionSpec as P

HEAD = 128
EPSILON = 1e-05
RINGX = 4
PEERS = 8
BF16 = jnp.bfloat16
VMEM_LIMIT = 46 * 1024 * 1024
F32 = jnp.float32
HBM = pl.BlockSpec(memory_space=pl.ANY)
NT = (((1,), (1,)), ((), ()))
NN = (((1,), (0,)), ((), ()))
TN = (((0,), (0,)), ((), ()))


def params():
    return pltpu.CompilerParams(
        dimension_semantics=("arbitrary",), vmem_limit_bytes=VMEM_LIMIT
    )


def cost(flops, nbytes):
    return pl.CostEstimate(flops=1, bytes_accessed=1, transcendentals=0)


def place(i, dx, dz):
    return ((i // 2 + dx) % RINGX) * 2 + ((i % 2) ^ dz)


def shift(array, dx, dz):
    return lax.ppermute(array, "tp", [(i, place(i, dx, dz)) for i in range(PEERS)])


def hop(array, by, cross):
    peers = lax.axis_size("section")
    pairs = [
        (i * PEERS + j, (i + by) * PEERS + (j ^ cross))
        for i in range(peers)
        if 0 <= i + by < peers
        for j in range(PEERS)
    ]
    return lax.ppermute(array, ("section", "tp"), pairs)


def partner_in(array, section):
    pairs = [(section * PEERS + j, section * PEERS + (j ^ 1)) for j in range(PEERS)]
    return lax.ppermute(array, ("section", "tp"), pairs)


def add(a, b):
    return (a.astype(F32) + b.astype(F32)).astype(BF16)


class Order:
    def __init__(self):
        self.token = jnp.zeros((), F32)

    def pin(self, *arrays):
        self.token, *arrays = lax.optimization_barrier((self.token, *arrays))
        return arrays if len(arrays) > 1 else arrays[0]


class Gather:
    def __init__(self, order, pair):
        self.order = order
        self.pair = order.pin(pair)
        far = shift(self.pair, 2, 0)
        self.rest = shift(self.pair, -1, 0), far, shift(self.pair, 1, 0)

    def done(self):
        return self.pair, *self.order.pin(*self.rest)


class GatherQuads:
    def __init__(self, order, own):
        self.order = order
        own = order.pin(own)
        far = shift(own, 2, 0)
        self.got = own, shift(own, -1, 0), far, shift(own, 1, 0)

    def second(self):
        self.quad = jnp.stack(self.order.pin(*self.got))
        self.other = shift(self.quad, 0, 1)

    def done(self):
        return self.quad, self.order.pin(self.other)


class ScatterSum:
    def __init__(self, order, far, plus, minus):
        self.order = order
        far, plus, minus = order.pin(far, plus, minus)
        self.got = shift(far, 2, 0), shift(plus, 1, 0), shift(minus, -1, 0)

    def done(self):
        return self.order.pin(*self.got)


class Hop:
    def __init__(self, order, part, by):
        self.order = order
        part = order.pin(part)
        self.got = hop(part, by, 0), hop(part, by, 1)

    def done(self, at_edge, edge_pair):
        same, cross = self.order.pin(*self.got)
        return jnp.where(at_edge, edge_pair, add(same, cross[::-1]))


def whole(array):
    zeros = (0,) * array.ndim
    return pl.BlockSpec(array.shape, lambda r, idx: zeros)


def per_head(heads, product):
    return jnp.concatenate([product(slice(h * HEAD, (h + 1) * HEAD)) for h in range(heads)], 0)


def softmax_scores(queries, keys, tokens, heads):
    scores = per_head(
        heads,
        lambda p: lax.dot_general(queries[:, p], keys[:, p], NT, preferred_element_type=F32),
    )
    scores = scores / math.sqrt(HEAD)
    rows = lax.broadcasted_iota(jnp.int32, scores.shape, 0) % tokens
    columns = lax.broadcasted_iota(jnp.int32, scores.shape, 1)
    scores = jnp.where(columns <= rows, scores, -1e30)
    raised = jnp.exp(scores - jnp.max(scores, -1, keepdims=True))
    return raised / jnp.sum(raised, -1, keepdims=True)


def row_block(tiles, k):
    return tiles.at[k]


def column_block(tiles, k):
    return tiles.at[PEERS + k]


def tile_call(w_value, w_out):
    width = w_value.shape[1]

    def body(w_value, w_out, tiles):
        tiles[0, 0] = w_value[...]
        tiles[1, 0] = w_out[...]

    tiles = pl.pallas_call(
        body,
        out_shape=jax.ShapeDtypeStruct((2, PEERS, width, width), BF16),
        grid=(PEERS,),
        in_specs=[
            pl.BlockSpec((width, width), lambda k: (k, 0)),
            pl.BlockSpec((width, width), lambda k: (0, k)),
        ],
        out_specs=pl.BlockSpec((2, 1, width, width), lambda k: (0, k, 0, 0)),
        compiler_params=params(),
        cost_estimate=cost(1, 1),
        name="weight_tiles",
    )(w_value, w_out)
    return tiles.reshape(2 * PEERS, width, width)


def stream_scratch(count, width):
    return [pltpu.VMEM((count, width, width), BF16), pltpu.SemaphoreType.DMA((count,))]


def wait_block(weight, blocks, sems, step, block_of):
    pltpu.make_async_copy(block_of(weight, 0), blocks.at[step], sems.at[step]).wait()


def layer_body(stashed, count, tokens, width, *refs):
    idx = refs[0]
    parts, pieces, rest = refs[1 : 1 + count], refs[-1], refs[1 + count : -1]
    gain, gain_own, key_row, weight = rest[:4]
    if stashed:
        out_values, out_probs, out_normed, out_centered, out_inv = rest[4:9]
    else:
        (out_mixed,) = rest[4:5]
    total, normed_own, mean_ref, inv_ref, weights, blocks, sems = rest[-7:]
    step = pl.program_id(0)
    full = width * PEERS
    heads = width // HEAD

    @pl.when(step == 0)
    def _():
        for k in range(PEERS):
            pltpu.make_async_copy(row_block(weight, idx[k]), blocks.at[k], sems.at[k]).start()
        for k in range(PEERS):
            pieces[k] = parts[k // 2][k % 2] if count == RINGX else parts[k % 2][k // 2]
        sums = jnp.zeros((tokens, HEAD), F32)
        squares = jnp.zeros((tokens, HEAD), F32)
        for r in range(PEERS):
            for c in range(heads):
                x = pieces[r, :, c * HEAD : (c + 1) * HEAD].astype(F32)
                sums += x
                squares += x * x
        mean = jnp.sum(sums, -1, keepdims=True) / full
        variance = jnp.sum(squares, -1, keepdims=True) / full - mean * mean
        mean_ref[...] = jnp.broadcast_to(mean, (tokens, HEAD))
        inv_ref[...] = jnp.broadcast_to(lax.rsqrt(variance + EPSILON), (tokens, HEAD))
        total[...] = jnp.zeros_like(total)
        mine = (pieces[idx[PEERS]].astype(F32) - mean_ref[:, :1]) * inv_ref[:, :1]
        normed_own[...] = (mine * gain_own[0]).astype(BF16)
        keys = (normed_own[...].astype(F32) * key_row[...]).astype(BF16)
        probs = softmax_scores(normed_own[...], keys, tokens, heads)
        if stashed:
            out_probs[...] = probs
            out_normed[...] = normed_own[...]
        else:
            weights[...] = probs.astype(BF16)

    centered = (pieces[step].astype(F32) - mean_ref[:, :1]) * inv_ref[:, :1]
    normed = (centered * gain[0]).astype(BF16)
    wait_block(weight, blocks, sems, step, row_block)
    total[...] += lax.dot_general(normed, blocks[step], NN, preferred_element_type=F32)

    if stashed:
        share = tokens // PEERS
        for dz in range(2):
            rows = pl.ds(pl.multiple_of(idx[PEERS + 1 + dz] * share, share), share)
            out_centered[dz, 0] = (
                pieces[step, rows, :].astype(F32) - mean_ref[rows, :1]
            ) * inv_ref[rows, :1]
            out_inv[dz] = inv_ref[rows, :]

    @pl.when(step == PEERS - 1)
    def _():
        values = total[...].astype(BF16)
        if stashed:
            out_values[...] = values
        else:
            for h in range(heads):
                part = slice(h * HEAD, (h + 1) * HEAD)
                out_mixed[:, part] = lax.dot_general(
                    weights[h * tokens : (h + 1) * tokens],
                    values[:, part],
                    NN,
                    preferred_element_type=F32,
                ).astype(BF16)


def layer_call(stashed, idx, pieces, gain, key_row, weight):
    count = len(pieces)
    tokens, width = pieces[0].shape[-2:]
    full = width * PEERS
    share = tokens // PEERS
    heads = width // HEAD
    if stashed:
        out_shape = (
            jax.ShapeDtypeStruct((tokens, width), BF16),
            jax.ShapeDtypeStruct((heads * tokens, tokens), F32),
            jax.ShapeDtypeStruct((tokens, width), BF16),
            jax.ShapeDtypeStruct((2, PEERS, share, width), F32),
            jax.ShapeDtypeStruct((2, share, HEAD), F32),
        )
        out_specs = (
            pl.BlockSpec((tokens, width), lambda r, idx: (0, 0)),
            pl.BlockSpec((heads * tokens, tokens), lambda r, idx: (0, 0)),
            pl.BlockSpec((tokens, width), lambda r, idx: (0, 0)),
            pl.BlockSpec((2, 1, share, width), lambda r, idx: (0, idx[r], 0, 0)),
            pl.BlockSpec((2, share, HEAD), lambda r, idx: (0, 0, 0)),
        )
    else:
        out_shape = jax.ShapeDtypeStruct((tokens, width), BF16)
        out_specs = pl.BlockSpec((tokens, width), lambda r, idx: (0, 0))

    def body(*refs):
        layer_body(stashed, count, tokens, width, *refs)

    scratch = [
        pltpu.VMEM((tokens, width), F32),
        pltpu.VMEM((tokens, width), BF16),
        pltpu.VMEM((tokens, HEAD), F32),
        pltpu.VMEM((tokens, HEAD), F32),
        pltpu.VMEM((heads * tokens, tokens), BF16),
    ] + stream_scratch(PEERS, width)
    scratch.append(pltpu.VMEM((PEERS, tokens, width), BF16))
    return pl.pallas_call(
        body,
        out_shape=out_shape,
        grid_spec=pltpu.PrefetchScalarGridSpec(
            num_scalar_prefetch=1,
            grid=(PEERS,),
            in_specs=[whole(p) for p in pieces]
            + [
                pl.BlockSpec((1, 1, width), lambda r, idx: (idx[r], 0, 0)),
                pl.BlockSpec((1, 1, width), lambda r, idx: (idx[PEERS + 1], 0, 0)),
                whole(key_row),
                HBM,
            ],
            out_specs=out_specs,
            scratch_shapes=scratch,
        ),
        compiler_params=params(),
        cost_estimate=cost(2 * tokens * full * width, 2 * full * width),
        name="stash_layer" if stashed else "mix_layer",
    )(idx, *pieces, gain, gain, key_row, weight)


def project_call(idx, mixed, tiles):
    tokens, width = mixed.shape
    order = (4, 5, 2, 3, 6, 7, 0, 1)

    def body(idx, mixed, tiles, far, plus, minus, here, blocks, sems):
        copies = [
            pltpu.make_async_copy(column_block(tiles, idx[r]), blocks.at[k], sems.at[k])
            for k, r in enumerate(order)
        ]
        for each in copies:
            each.start()
        for k in range(len(order)):
            copies[k].wait()
            (far, plus, minus, here)[k // 2][k % 2] = lax.dot_general(
                mixed[...], blocks[k], NN, preferred_element_type=F32
            ).astype(BF16)

    pair = pl.BlockSpec((2, tokens, width), lambda r, idx: (0, 0, 0))
    return pl.pallas_call(
        body,
        out_shape=[jax.ShapeDtypeStruct((2, tokens, width), BF16)] * RINGX,
        grid_spec=pltpu.PrefetchScalarGridSpec(
            num_scalar_prefetch=1,
            grid=(1,),
            in_specs=[whole(mixed), HBM],
            out_specs=[pair] * RINGX,
            scratch_shapes=stream_scratch(PEERS, width),
        ),
        compiler_params=params(),
        cost_estimate=cost(16 * tokens * width * width, 16 * width * width),
        name="project",
    )(idx, mixed, tiles)


def sent_call(plan, place, held):
    _, tokens, width = held.shape
    steps = plan.shape[1]

    def body(plan, place, held, out):
        out[...] = held[...]

    def slot(t, plan, place):
        return plan[(place[0] * steps + t) * 2 + 1], 0, 0

    return pl.pallas_call(
        body,
        out_shape=jax.ShapeDtypeStruct((steps, tokens, width), BF16),
        grid_spec=pltpu.PrefetchScalarGridSpec(
            num_scalar_prefetch=2,
            grid=(steps,),
            in_specs=[pl.BlockSpec((1, tokens, width), slot)],
            out_specs=pl.BlockSpec((1, tokens, width), lambda t, plan, place: (t, 0, 0)),
        ),
        compiler_params=params(),
        cost_estimate=cost(1, 1),
        name="sent_blocks",
    )(plan.reshape(-1), place, held)


def chosen_call(plan, place, held, got, first):
    count, tokens, width = got.shape
    steps = plan.shape[1]

    def body(plan, place, held, got, out):
        side = plan[(place[1] * steps + first + pl.program_id(0)) * 2]

        @pl.when(side == 0)
        def _():
            out[...] = held[...]

        @pl.when(side != 0)
        def _():
            out[...] = got[...]

    def slot(t, plan, place):
        return plan[(place[1] * steps + first + t) * 2 + 1], 0, 0

    block = pl.BlockSpec((1, tokens, width), lambda t, plan, place: (t, 0, 0))
    return pl.pallas_call(
        body,
        out_shape=jax.ShapeDtypeStruct(got.shape, BF16),
        grid_spec=pltpu.PrefetchScalarGridSpec(
            num_scalar_prefetch=2,
            grid=(count,),
            in_specs=[pl.BlockSpec((1, tokens, width), slot), block],
            out_specs=block,
        ),
        compiler_params=params(),
        cost_estimate=cost(1, 1),
        name="chosen_blocks",
    )(plan.reshape(-1), place, held, got)


def attention_grad_call(idx, pieces, stashed, key_row, weight):
    share, width = pieces[0].shape[-2:]
    tokens = share * PEERS
    full = width * PEERS
    values, probs, normed = stashed

    def body(
        idx, pair, plus, far, minus, values, probs, normed, key_row,
        weight, out_values, out_direct, grads, total, sort_values, sort_direct, blocks, sems,
    ):
        step = pl.program_id(0)
        heads = width // HEAD

        def rows(r):
            return pl.ds(pl.multiple_of(idx[r] * share, share), share)

        @pl.when(step == 0)
        def _():
            for k in range(PEERS):
                pltpu.make_async_copy(
                    column_block(weight, k), blocks.at[k], sems.at[k]
                ).start()
            for k, part in enumerate((pair, plus, far, minus)):
                for dz in range(2):
                    for c in range(PEERS):
                        grads[c, rows(2 * k + dz)] = part[dz, c]
            total[...] = jnp.zeros_like(total)

        wait_block(weight, blocks, sems, step, column_block)
        total[...] += lax.dot_general(
            grads[step], blocks[step], NT, preferred_element_type=F32
        )

        @pl.when(step == PEERS - 1)
        def _():
            grad_mixed = total[...].astype(BF16)
            grad_probs = per_head(
                heads,
                lambda p: lax.dot_general(
                    grad_mixed[:, p], values[:, p], NT, preferred_element_type=F32
                ),
            )
            weights = probs[...]
            grad_scores = (
                weights
                * (grad_probs - jnp.sum(grad_probs * weights, -1, keepdims=True))
                / math.sqrt(HEAD)
            ).astype(BF16)
            weights = weights.astype(BF16)
            queries = normed[...]
            keys = (queries.astype(F32) * key_row[...]).astype(BF16)
            for h in range(heads):
                part = slice(h * HEAD, (h + 1) * HEAD)
                rows_of = slice(h * tokens, (h + 1) * tokens)
                grad_values = lax.dot_general(
                    weights[rows_of], grad_mixed[:, part], TN, preferred_element_type=F32
                )
                grad_query = lax.dot_general(
                    grad_scores[rows_of], keys[:, part], NN, preferred_element_type=F32
                )
                grad_keys = lax.dot_general(
                    grad_scores[rows_of], queries[:, part], TN, preferred_element_type=F32
                )
                sort_values[:, part] = grad_values.astype(BF16)
                sort_direct[:, part] = grad_query + grad_keys * key_row[:, part]
            for r in range(PEERS):
                out_values[r * share : (r + 1) * share] = sort_values[rows(r)]
                out_direct[r * share : (r + 1) * share] = sort_direct[rows(r)]

    result = pl.BlockSpec((tokens, width), lambda r, idx: (0, 0))
    return pl.pallas_call(
        body,
        out_shape=(
            jax.ShapeDtypeStruct((tokens, width), BF16),
            jax.ShapeDtypeStruct((tokens, width), F32),
        ),
        grid_spec=pltpu.PrefetchScalarGridSpec(
            num_scalar_prefetch=1,
            grid=(PEERS,),
            in_specs=[whole(p) for p in pieces]
            + [whole(values), whole(probs), whole(normed), whole(key_row)]
            + [HBM],
            out_specs=(result, result),
            scratch_shapes=[
                pltpu.VMEM((PEERS, tokens, width), BF16),
                pltpu.VMEM((tokens, width), F32),
                pltpu.VMEM((tokens, width), BF16),
                pltpu.VMEM((tokens, width), F32),
            ]
            + stream_scratch(PEERS, width),
        ),
        compiler_params=params(),
        cost_estimate=cost(2 * tokens * full * width, 2 * full * width),
        name="attention_grad",
    )(idx, *pieces, values, probs, normed, key_row, weight)


def back_project_call(idx, grad_values, direct, weight):
    tokens, width = grad_values.shape
    full = width * PEERS
    share = tokens // PEERS

    def body(
        idx, grad_values, direct, weight, here, plus, far, minus, blocks, sems
    ):
        step = pl.program_id(0)

        @pl.when(step == 0)
        def _():
            for k in range(PEERS):
                pltpu.make_async_copy(row_block(weight, k), blocks.at[k], sems.at[k]).start()

        wait_block(weight, blocks, sems, step, row_block)
        product = lax.dot_general(
            grad_values[...], blocks[step], NT, preferred_element_type=F32
        )
        mine = (step == idx[0]).astype(F32)
        product = (product + direct[...] * mine).astype(BF16)

        def piece(r):
            return product[r * share : (r + 1) * share]

        for k, part in enumerate((here, plus, far, minus)):
            for dz in range(2):
                part[dz, 0] = piece(2 * k + dz)

    return pl.pallas_call(
        body,
        out_shape=[jax.ShapeDtypeStruct((2, PEERS, share, width), BF16)] * RINGX,
        grid_spec=pltpu.PrefetchScalarGridSpec(
            num_scalar_prefetch=1,
            grid=(PEERS,),
            in_specs=[
                pl.BlockSpec((tokens, width), lambda c, idx: (0, 0)),
                pl.BlockSpec((tokens, width), lambda c, idx: (0, 0)),
                HBM,
            ],
            scratch_shapes=stream_scratch(PEERS, width),
            out_specs=[pl.BlockSpec((2, 1, share, width), lambda c, idx: (0, c, 0, 0))] * RINGX,
        ),
        compiler_params=params(),
        cost_estimate=cost(2 * tokens * full * width, 2 * full * width),
        name="back_project",
    )(idx, grad_values, direct, weight)


def norm_grad_call(parts, gain, centered, inv_std, grad_own, last=False):
    _, blocks, share, width = parts[0].shape
    full = blocks * width

    def body(*refs):
        parts, (gain, centered, inv_std, grad_own, out) = refs[:RINGX], refs[RINGX:]
        for dz in range(2):
            scaled = sum(part[dz].astype(F32) for part in parts) * gain[...]
            mid = centered[dz]
            first = jnp.sum(jnp.sum(scaled, 0), -1, keepdims=True) / full
            second = jnp.sum(jnp.sum(scaled * mid, 0), -1, keepdims=True) / full
            result = inv_std[dz][:, :1][None] * (scaled - first[None] - mid * second[None])
            if dz == 0:
                result = result + grad_own[...].astype(F32)
            if last:
                out[:, dz] = result.astype(BF16)
            else:
                out[dz] = result.astype(BF16)

    shape = (blocks, 2, share, width) if last else parts[0].shape
    return pl.pallas_call(
        body,
        out_shape=jax.ShapeDtypeStruct(shape, BF16),
        compiler_params=pltpu.CompilerParams(vmem_limit_bytes=VMEM_LIMIT),
        cost_estimate=cost(1, 1),
        name="norm_grad",
    )(*parts, gain, centered, inv_std, grad_own)


def swap_layout(array):
    return lax.all_to_all(array, "tp", split_axis=0, concat_axis=0, tiled=True)


def per_device(
    inputs, cotangents, carried, pending, stash, stash_plan, gain, key_gain, w_value, w_out
):
    steps = inputs.shape[0] + 1
    tokens = carried.shape[1]
    width = key_gain.shape[-1]
    share = tokens // PEERS
    me = lax.axis_index("tp")
    places = [place(me, r // 2, r % 2) for r in range(PEERS)]
    relative = jnp.stack(places + [jnp.zeros_like(me), me, me ^ 1]).astype(jnp.int32)
    section = lax.axis_index("section")
    sections = lax.axis_size("section")
    mirror = sections - 1 - section
    gain_blocks = gain[0].reshape(PEERS, 1, width)
    held = stash[0]
    place_of = jnp.stack([mirror, section]).astype(jnp.int32)

    order = Order()
    pin = order.pin

    def from_mirror(array):
        return lax.ppermute(array, "section", [(i, sections - 1 - i) for i in range(sections)])

    def finished(parts):
        own = jnp.stack([p[0] for p in parts])
        return own, shift(pin(jnp.stack([p[1] for p in parts])), 0, 1)

    def mix(pieces):
        mixed = pin(layer_call(False, relative, pin(*pieces), gain_blocks, key_gain, tiles))
        far, plus, minus, here = pin(*project_call(relative, mixed, tiles))
        return ScatterSum(order, far, plus, minus), here

    def stash_layer(idx, pieces):
        pieces = pin(*pieces)
        pieces = pieces if isinstance(pieces, list) else [pieces]
        return pin(*layer_call(True, idx, pieces, gain_blocks, key_gain, tiles))

    is_first = section == 0
    is_last = section == sections - 1
    residual_place = (jnp.arange(2) == 0).astype(F32)[:, None, None]

    spread = swap_layout(
        pin(
            jnp.concatenate([pending, cotangents])
            .reshape(steps, PEERS, share, width)
            .transpose(1, 0, 2, 3)
        )
    )
    own = pin(carried[0])
    partner = shift(own, 0, 1)
    sent = pin(sent_call(stash_plan, place_of, held))
    mirrored = from_mirror(sent[:1])
    tiles = pin(tile_call(*pin(w_value[0], w_out[0])))
    fwd_pair = jnp.stack([own, pin(partner)])
    fwd_gather = Gather(order, fwd_pair)
    stash_own = pin(chosen_call(stash_plan, place_of, held, pin(mirrored), 0))[0]
    stash_partner = shift(stash_own, 0, 1)
    spread = pin(spread).transpose(1, 0, 2, 3)
    grad_own = pin(spread[0])
    grad_partner = shift(grad_own, 0, 1)
    stash_gather = Gather(order, jnp.stack([stash_own, pin(stash_partner)]))
    fwd_sums, here = mix(fwd_gather.done())
    grad_pair = jnp.stack([grad_own, pin(grad_partner)])
    grad_gather = Gather(order, grad_pair)
    late = from_mirror(pin(sent[1:]))

    forward_parts = []
    backward_parts = []
    for t in range(steps):
        if t > 0:
            backward_parts.append(
                pin(
                    norm_grad_call(
                        (here_grad, *grad_sums.done()),
                        gain_blocks,
                        centered,
                        inv_std,
                        grad_pair[0],
                    )
                )
            )
            grad_hop = Hop(order, backward_parts[-1], -1)
        else:
            stashed = stash_layer(relative, stash_gather.done())
            grad_pieces = grad_gather.done()
            values, probs, normed, centered, inv_std = stashed
            grad_values, direct = pin(
                *attention_grad_call(
                    relative, grad_pieces, (values, probs, normed), key_gain, tiles
                )
            )
        forward_parts.append(
            (
                sum(part.astype(F32) for part in (here, *fwd_sums.done()))
                + fwd_pair[:1].astype(F32) * residual_place
            ).astype(BF16)
        )
        if t + 1 < steps:
            fwd_hop = Hop(order, forward_parts[-1], 1)
        else:
            forward_last = finished(forward_parts[-1:])
        if t > 0:
            stashed = stash_layer(relative, stash_gather.done())
            grad_pair = grad_hop.done(is_last, cotangent_pairs[t - 1])
            grad_gather = Gather(order, grad_pair)
        else:
            late = pin(chosen_call(stash_plan, place_of, held, pin(late), 1))
            input_pairs = jnp.stack([inputs, partner_in(pin(inputs), 0)], 1)
            cotangent_pairs = jnp.stack(
                [spread[1:], partner_in(pin(spread[1:]), sections - 1)], 1
            )
        if t == 0:
            here_grad, plus, far, minus = pin(
                *back_project_call(relative, *pin(grad_values, direct), tiles)
            )
            grad_sums = ScatterSum(order, far, plus, minus)
        if t + 1 == steps:
            forward_early = finished(forward_parts[:-1])
            backward_early = finished(backward_parts)
        if t > 0:
            grad_pieces = grad_gather.done()
        if t > 0:
            values, probs, normed, centered, inv_std = stashed
            grad_values, direct = pin(
                *attention_grad_call(
                    relative, grad_pieces, (values, probs, normed), key_gain, tiles
                )
            )
        if t + 1 < steps:
            fwd_pair = fwd_hop.done(is_first, input_pairs[t])
            fwd_gather = Gather(order, fwd_pair)
        if t > 0:
            here_grad, plus, far, minus = pin(
                *back_project_call(relative, *pin(grad_values, direct), tiles)
            )
        if t + 1 < steps:
            stash_gather = GatherQuads(order, late[t])
        if t > 0:
            grad_sums = ScatterSum(order, far, plus, minus)
        if t + 1 < steps:
            pieces = fwd_gather.done()
            fwd_sums, here = mix(pieces)
            stash_gather.second()

    early = add(*pin(*backward_early)).transpose(1, 0, 2, 3)
    early = swap_layout(pin(early))
    last_part = norm_grad_call(
        (here_grad, *grad_sums.done()), gain_blocks, centered, inv_std, grad_pair[0], True
    )
    last = swap_layout(last_part).reshape(RINGX, 2, 2, share, width)
    last = add(last[:, :, 0], last[:, ::-1, 1]).reshape(1, PEERS, share, width)
    forward = jnp.concatenate([add(*forward_early), add(*forward_last)])
    backward = jnp.concatenate([early.transpose(1, 0, 2, 3), last])
    return (forward[None], backward.reshape(1, steps, tokens, width))


def solution(mesh):
    return jax.shard_map(
        per_device,
        mesh=mesh,
        in_specs=(
            P(None, None, "tp"),
            P(None, None, "tp"),
            P("section", None, "tp"),
            P("section", None, "tp"),
            P("section", None, None, "tp"),
            P(),
            P("section", None),
            P("section", "tp"),
            P("section", None, "tp"),
            P("section", "tp", None),
        ),
        out_specs=(P("section", None, None, "tp"), P("section", None, None, "tp")),
        check_vma=False,
    )
```
